256 devices in a mesh: row: 16 (over z_hi, x), col: 16 (over z_lo, y, core).
Axes of the slice: x: 4, y: 4, z: 8 (z_hi: 4, z_lo: 2; z = z_hi * 2 + z_lo), core: 2. Of those that a mesh axis runs over, the one named last changes fastest.
Arguments:
- density: float32 [16, 16, 18, 128, 128], P('row', 'col'), as said below
- tile_coords: int32 [16, 16, 18, 2], replicated, may hold values from 0 to 511, as said below
Outputs:
- purified: float32 [16, 16, 18, 128, 128], P('row', 'col')
- mean_diagonal: float32 [], replicated
The draws below stay inside these ranges and needn't reach their ends.
Inputs may be any that keep to these rules, and one draw needn't show every extreme that they name: `tile_coords`: slot t of device (r, c) names a block (I, J) with (I div (size of axis col)) mod (size of axis row) = r and c = pi(J mod (size of axis col)) for one permutation pi of 0 to (size of axis col) - 1, the same for all blocks; every slot is filled. Each present block is named once. Block (I, J) is present exactly when (J - I) mod 512 lies in a set of 9 offsets that holds 0 and is closed under negation, so the pattern is symmetric and every block row holds 9 blocks. No device names two blocks of one block row. density[r, c, t] is the block named by tile_coords[r, c, t]; the blocks form a symmetric matrix (block (J, I) is the transpose of block (I, J)).
All inputs are finite; a program needn't handle non-finite values.
Results may differ from the reference program's by a relative error of at most 0.025.
Values may be sent and summed in bfloat16 or wider, within the bound.
A program may use at most 128 MiB of HBM per device.

```python
import jax
import jax.numpy as jnp
from jax import lax

NB = 512
BLK = 128
OFFSETS = 9
TILES = 18
N_ROW = 16
N_COL = 16


def block_layout(key):
    smaller = min(N_ROW, N_COL)
    half_count = (OFFSETS - 1) // 2
    key_a, key_b, key_c, key_d = jax.random.split(key, 4)
    residues = jax.random.permutation(key_a, smaller // 2 - 1)[:half_count] + 1
    multiples = jax.random.randint(key_b, (half_count,), 0, NB // smaller)
    multiples = multiples.at[0].set(0)
    if half_count >= 2:
        multiples = multiples.at[half_count - 1].set(N_ROW // 2)
    distance = (residues + smaller * multiples).astype(jnp.int32)
    offsets = jnp.concatenate([jnp.zeros((1,), jnp.int32), distance, NB - distance]).astype(jnp.int32)
    shuffle = jax.random.permutation(key_d, N_COL).astype(jnp.int32)
    first_res = residues[0] % N_COL
    wanted = (shuffle[0] + N_COL // 2) % N_COL
    where_wanted = jnp.argmax((shuffle == wanted).astype(jnp.int32)).astype(jnp.int32)
    held = shuffle[first_res]
    shuffle = shuffle.at[where_wanted].set(held)
    shuffle = shuffle.at[first_res].set(wanted)
    rows = jnp.repeat(jnp.arange(NB, dtype=jnp.int32), OFFSETS)
    cols = (rows + jnp.tile(offsets, NB)) % NB
    total = NB * OFFSETS
    device = rows // N_COL % N_ROW * N_COL + shuffle[cols % N_COL]
    scores = jax.random.permutation(key_c, total).astype(jnp.int32)
    order = jnp.argsort(device * total + scores)
    device_sorted = device[order]
    counts = jax.ops.segment_sum(jnp.ones((total,), jnp.int32), device, num_segments=N_ROW * N_COL)
    starts = jnp.cumsum(counts) - counts
    slot = jnp.arange(total, dtype=jnp.int32) - starts[device_sorted]
    table = jnp.full((N_ROW * N_COL, TILES, 2), -1, jnp.int32)
    table = table.at[device_sorted, slot].set(jnp.stack([rows[order], cols[order]], axis=-1))
    return table.reshape(N_ROW, N_COL, TILES, 2)


def draw_tile_coords(key, part):
    table = block_layout(key)
    return table


def draw_density(key, part):
    table = block_layout(key)
    key = jax.random.fold_in(key, 7)
    flat = table.reshape(-1, 2)
    row_ids = flat[:, 0]
    col_ids = flat[:, 1]
    pair_ids = jnp.minimum(row_ids, col_ids) * NB + jnp.maximum(row_ids, col_ids)
    spread = 0.7 * float(OFFSETS * BLK) ** (-0.375)
    block_key = jax.random.fold_in(key, 1)

    def single(pair, row_id, col_id):
        sub = jax.random.fold_in(block_key, pair)
        noise = jax.random.truncated_normal(sub, -4.0, 4.0, (BLK, BLK), jnp.float32)
        noise = jnp.where(row_id > col_id, noise.T, noise)
        klass = (jnp.maximum(row_id, 0) // N_COL % N_ROW).astype(jnp.float32)
        level = 0.3 + 0.4 * klass / float(N_ROW - 1)
        diagonal = level * jnp.eye(BLK, dtype=jnp.float32) + spread * 0.70710678 * (noise + noise.T)
        block = jnp.where(row_id == col_id, diagonal, spread * noise)
        return jnp.where(row_id >= 0, block, jnp.zeros_like(block))
    tiles = jax.vmap(single)(pair_ids, row_ids, col_ids)
    return tiles.reshape(N_ROW, N_COL, TILES, BLK, BLK).astype(jnp.float32)


def setup_inputs(seed: int = 0) -> dict:
    seeds = jax.random.split(jax.random.key(seed), 3)
    return {
        "density": draw_density(jax.random.fold_in(seeds[2], 71), 0),
        "tile_coords": draw_tile_coords(jax.random.fold_in(seeds[2], 71), 0),
    }


def block_product(left, right, coords, row_list, slot_map):
    count = coords.shape[0]

    def single(target):
        row_id = coords[target, 0]
        col_id = coords[target, 1]
        slots = row_list[jnp.maximum(row_id, 0)]
        inner = coords[slots, 1]
        partner = slot_map[inner * NB + jnp.maximum(col_id, 0)]
        left_rows = left[slots].astype(jnp.float32)
        right_rows = right[partner].astype(jnp.float32)
        terms = jnp.einsum("mik,mkj->mij", left_rows, right_rows, precision=lax.Precision.HIGHEST)
        rounded = lax.optimization_barrier(terms.astype(jnp.bfloat16)).astype(jnp.float32)
        summed = jnp.sum(rounded, axis=0)
        return jnp.where(row_id >= 0, summed, jnp.zeros_like(summed))

    return lax.map(single, jnp.arange(count, dtype=jnp.int32))


def reference(density, tile_coords):
    tiles = density.reshape(-1, BLK, BLK)
    coords = tile_coords.reshape(-1, 2).astype(jnp.int32)
    count = tiles.shape[0]
    valid = coords[:, 0] >= 0
    keys = jnp.where(valid, coords[:, 0] * NB + coords[:, 1], NB * NB).astype(jnp.int32)
    slot_map = jnp.full((NB * NB,), count, jnp.int32).at[keys].set(jnp.arange(count, dtype=jnp.int32), mode="drop")
    order = jnp.argsort(keys).astype(jnp.int32)
    row_list = order[:NB * OFFSETS].reshape(NB, OFFSETS)
    blank = jnp.zeros((1, BLK, BLK), jnp.bfloat16)
    dense_b = jnp.concatenate([tiles.astype(jnp.bfloat16), blank], axis=0)
    square = block_product(dense_b, dense_b, coords, row_list, slot_map)
    square_b = jnp.concatenate([square.astype(jnp.bfloat16), blank], axis=0)
    cube = block_product(square_b, dense_b, coords, row_list, slot_map)
    purified = 3.0 * square - 2.0 * cube
    diagonal = valid & (coords[:, 0] == coords[:, 1])
    traces = jnp.einsum("nii->n", purified)
    mean_diagonal = jnp.sum(jnp.where(diagonal, traces, jnp.zeros_like(traces))) / (NB * BLK)
    return purified.reshape(density.shape), mean_diagonal
```

```python
import jax
import jax.numpy as jnp
from jax import lax
from jax.experimental import pallas as pl
from jax.experimental.pallas import tpu as pltpu
from jax.sharding import PartitionSpec as P

NB = 512
BLK = 128
TILES = 18
PACK = BLK + 16
BF = jnp.bfloat16
F32 = jnp.float32
MESH = pl.DeviceIdType.MESH

CHIP_STEPS = ((0, 1), (0, 3), (1, 0), (0, 2), (1, 1), (1, 3), (1, 2))
RING_STEPS = (1, 3, 2)

SRC, DIDX, EIDX, DIAG, TABLE = 0, 32, 64, 96, 128


def dot(a, b):
    return jnp.dot(a, b, preferred_element_type=F32)


def dot_t(a, b):
    return lax.dot_general(a, b, (((1,), (1,)), ((), ())), preferred_element_type=F32)


def grids():
    row = lax.broadcasted_iota(jnp.int32, (BLK, BLK), 0)
    col = lax.broadcasted_iota(jnp.int32, (BLK, BLK), 1)
    return row, col


def pack(first, second):
    row, col = grids()
    body = jnp.where(row <= col, first, second)
    diag = jnp.sum(jnp.where(row == col, second, 0.0), axis=0, keepdims=True)
    return body, jnp.broadcast_to(diag, (PACK - BLK, BLK))


def unpack(body, diag):
    row, col = grids()
    turned = body.T
    first = jnp.where(row <= col, body, turned)
    second = jnp.where(row > col, body, jnp.where(row < col, turned, diag))
    return first, second


def kernel(
    table, dens_hbm, out_hbm, special, trace,
    dens, tiles, terms, dpack, epack, spack, mine, twins, summed, landed, sums,
    dfull, efull, sfull, square, outs, tcol, trow,
    load_sem, d_send, d_recv, e_send, e_recv, s_send, s_recv,
    x_send, x_recv, r_send, r_recv, tc_send, tc_recv, tr_send, tr_recv, out_sem,
):
    me_r = lax.axis_index("row")
    me_c = lax.axis_index("col")
    core = lax.rem(me_c, 2)
    other = 1 - core
    chip = me_c // 2
    zlo, y = chip // 4, lax.rem(chip, 4)
    zhi, x = me_r // 4, lax.rem(me_r, 4)
    twin = chip * 2 + other
    chips = [lax.rem(zlo + dz, 2) * 4 + lax.rem(y + dy, 4) for dz, dy in CHIP_STEPS]
    zs = [lax.rem(zhi + d, 4) for d in RING_STEPS]
    xs = [lax.rem(x + d, 4) for d in RING_STEPS]

    barrier = pltpu.get_barrier_semaphore()
    load = pltpu.make_async_copy(dens_hbm, dens, load_sem)
    load.start()

    @pl.loop(1, 16)
    def _(i):
        pl.semaphore_signal(barrier, inc=1, device_id={"col": lax.rem(me_c + i, 16)}, device_id_type=MESH)
        pl.semaphore_signal(barrier, inc=1, device_id={"row": lax.rem(me_r + i, 16)}, device_id_type=MESH)

    def to_col(src, dst, send, recv, c):
        return pltpu.make_async_remote_copy(
            src_ref=src, dst_ref=dst, send_sem=send, recv_sem=recv,
            device_id={"col": c}, device_id_type=MESH,
        )

    def to_row(src, dst, send, recv, r):
        return pltpu.make_async_remote_copy(
            src_ref=src, dst_ref=dst, send_sem=send, recv_sem=recv,
            device_id={"row": r}, device_id_type=MESH,
        )

    def spread_start(buf, send, recv):
        own = buf.at[core, chip]
        for n, ch in enumerate(chips):
            to_col(own, own, send.at[n], recv.at[core, chip], ch * 2 + core).start()
        to_col(own, own, send.at[7], recv.at[core, chip], twin).start()

    def spread_forward(buf, send, recv, n):
        part = buf.at[core, chips[n]]
        copy = to_col(part, part, send.at[8 + n], recv.at[core, chips[n]], twin)
        copy.wait_recv()
        copy.start()

    def spread_twin(buf, send, recv, ch):
        part = buf.at[other, ch]
        to_col(part, part, send.at[0], recv.at[other, ch], twin).wait_recv()

    def spread_end(buf, send, recv):
        own = buf.at[core, chip]
        for n in range(15):
            to_col(own, own, send.at[n], recv.at[core, chip], twin).wait_send()

    def reduce_pack(skip_own, which):
        @pl.loop(0, 8)
        def _(k):
            i0 = table[SRC + (which * 8 + k) * 2]
            i1 = table[SRC + (which * 8 + k) * 2 + 1]
            if skip_own:
                own = jnp.logical_and(which == core, k == chip)
                i0 = jnp.where(own, TILES, i0)
                i1 = jnp.where(own, TILES, i1)
            body, diag = pack(terms[i0].astype(F32), terms[i1].astype(F32))
            mine[which, k, 0:BLK] = body.astype(BF)
            mine[which, k, BLK:PACK] = diag.astype(BF)

    def twin_copy(s):
        return to_col(mine.at[other], twins.at[s], x_send.at[s], x_recv.at[s], twin)

    def reduce_send(s):
        twin_copy(s).wait_recv()

        @pl.loop(0, 8)
        def _(k):
            summed[s, k] = (mine[core, k].astype(F32) + twins[s, k].astype(F32)).astype(BF)

        for n, ch in enumerate(chips):
            to_col(summed.at[s, ch], landed.at[s, chip], r_send.at[s, n], r_recv.at[s, chip], ch * 2 + core).start()

    def reduce_end(s):
        total = summed[s, chip].astype(F32)
        for n, ch in enumerate(chips):
            to_col(summed.at[s, ch], landed.at[s, ch], r_send.at[s, n], r_recv.at[s, ch], ch * 2 + core).wait_recv()
            total = total + landed[s, ch].astype(F32)
        sums[s] = total

    load.wait()

    @pl.loop(0, TILES)
    def _(t):
        tiles[t] = dens[t].astype(BF)

    zero = jnp.zeros((BLK, BLK), BF)
    tiles[TILES] = zero
    terms[TILES] = zero
    my_pos = (core * 8 + chip) * 2
    own0 = table[SRC + my_pos]
    own1 = table[SRC + my_pos + 1]
    body, diag = pack(tiles[own0].astype(F32), tiles[own1].astype(F32))
    body, diag = body.astype(BF), diag.astype(BF)
    dpack[core, chip, 0:BLK] = body
    dpack[core, chip, BLK:PACK] = diag
    epack[zhi, x, 0:BLK] = body
    epack[zhi, x, BLK:PACK] = diag

    pl.semaphore_wait(barrier, 30)

    def along_z(n):
        own = epack.at[zhi, x]
        return to_row(own, own, e_send.at[n], e_recv.at[zhi, x], zs[n] * 4 + x)

    def along_x(z, m, n):
        part = epack.at[z, x]
        return to_row(part, part, e_send.at[m], e_recv.at[z, x], zhi * 4 + xs[n])

    for n in range(3):
        along_z(n).start()
    for n in range(3):
        along_x(zhi, 3 + n, n).start()
    spread_start(dpack, d_send, d_recv)

    @pl.loop(0, TILES)
    def _(t):
        b = tiles[t]
        terms[t] = dot_t(b, b).astype(BF)

    reduce_pack(False, other)
    twin_copy(0).start()
    reduce_pack(False, core)

    for n in range(3):
        part = epack.at[zs[n], x]
        to_row(part, part, e_send.at[0], e_recv.at[zs[n], x], me_r).wait_recv()
        for m in range(3):
            along_x(zs[n], 6 + 3 * n + m, m).start()

    reduce_send(0)

    def expand(buf, which, k, full, at):
        first, second = unpack(buf[which, k, 0:BLK].astype(F32), buf[which, k, BLK:BLK + 1].astype(F32))
        full[at] = first.astype(BF)
        full[at + 1] = second.astype(BF)

    for n in range(7):
        spread_forward(dpack, d_send, d_recv, n)

    @pl.loop(0, 8)
    def _(k):
        expand(dpack, core, k, dfull, (core * 8 + k) * 2)

    reduce_end(0)
    total = sums[0]
    spack[core, chip] = total.astype(BF)
    spread_start(spack, s_send, s_recv)

    for ch in range(8):
        spread_twin(dpack, d_send, d_recv, ch)

    @pl.loop(0, 8)
    def _(k):
        expand(dpack, other, k, dfull, (other * 8 + k) * 2)

    @pl.loop(0, TILES)
    def _(t):
        square[t] = dot(dfull[table[DIDX + t]], tiles[t])

    for n in range(3):
        part = epack.at[zhi, xs[n]]
        to_row(part, part, e_send.at[0], e_recv.at[zhi, xs[n]], me_r).wait_recv()
    for m in range(3):
        for n in range(3):
            part = epack.at[zs[m], xs[n]]
            to_row(part, part, e_send.at[0], e_recv.at[zs[m], xs[n]], me_r).wait_recv()

    @pl.loop(0, 4)
    def _(z):
        for k in range(4):
            expand(epack, z, k, efull, (z * 4 + k) * 2)

    twin_copy(0).wait_send()

    @pl.loop(0, TILES)
    def _(t):
        b = tiles[t]
        f = dot(b, efull[table[EIDX + t]])
        square[t] = square[t] + f
        terms[t] = dot_t(f.astype(BF), b).astype(BF)

    reduce_pack(True, other)
    twin_copy(1).start()
    reduce_pack(True, core)

    def fold(v):
        return jnp.sum(v.reshape(BLK // 8, 8, BLK), axis=0)

    def step(t, acc):
        b = tiles[t]
        s = square[t]
        low = s.astype(BF)
        outs[t] = 3.0 * s - 2.0 * dot(low, efull[table[EIDX + t]])
        wide = b.astype(F32)
        off = (1 - table[DIAG + t]).astype(F32)
        return acc + fold(wide * (3.0 * wide - (2.0 * off) * low.astype(F32)))

    acc = lax.fori_loop(0, TILES, step, jnp.zeros((8, BLK), F32))

    s0, s1 = unpack(sums[0, 0:BLK], sums[0, BLK:BLK + 1])
    for h, s in ((0, s0), (1, s1)):
        d = tiles[own0 if h == 0 else own1]
        low = s.astype(BF)
        rest = (s - dot(d, d)).astype(BF)
        special[h] = 3.0 * s - 2.0 * (dot(d, rest) + dot(low, d))
        acc = acc - 2.0 * fold(low.astype(F32) * d.astype(F32))
    tcol[me_c] = acc

    reduce_send(1)

    @pl.loop(1, 16)
    def _(i):
        to_col(tcol.at[me_c], tcol.at[me_c], tc_send.at[i], tc_recv.at[me_c], lax.rem(me_c + i, 16)).start()

    for n in range(7):
        spread_forward(spack, s_send, s_recv, n)

    @pl.loop(0, 8)
    def _(k):
        expand(spack, core, k, sfull, (core * 8 + k) * 2)

    for ch in range(8):
        spread_twin(spack, s_send, s_recv, ch)

    @pl.loop(0, 8)
    def _(k):
        expand(spack, other, k, sfull, (other * 8 + k) * 2)

    @pl.loop(1, 16)
    def _(i):
        c = lax.rem(me_c + i, 16)
        to_col(tcol.at[c], tcol.at[c], tc_send.at[i], tc_recv.at[c], c).wait_recv()

    trow[me_r] = jnp.sum(tcol[...], axis=0)

    @pl.loop(1, 16)
    def _(i):
        to_row(trow.at[me_r], trow.at[me_r], tr_send.at[i], tr_recv.at[me_r], lax.rem(me_r + i, 16)).start()

    @pl.loop(0, TILES)
    def _(t):
        outs[t] = outs[t] - 2.0 * dot(sfull[table[DIDX + t]], tiles[t])

    store = pltpu.make_async_copy(outs, out_hbm, out_sem)
    store.start()

    reduce_end(1)
    q0, q1 = unpack(sums[1, 0:BLK], sums[1, BLK:BLK + 1])
    special[0] = special[0] - 2.0 * q0
    special[1] = special[1] - 2.0 * q1

    @pl.loop(1, 16)
    def _(i):
        r = lax.rem(me_r + i, 16)
        to_row(trow.at[r], trow.at[r], tr_send.at[i], tr_recv.at[r], r).wait_recv()

    trace[0, 0] = jnp.sum(trow[...]) / (NB * BLK)

    spread_end(dpack, d_send, d_recv)
    spread_end(spack, s_send, s_recv)
    own = epack.at[zhi, x]
    for n in range(15):
        to_row(own, own, e_send.at[n], e_recv.at[zhi, x], me_r).wait_send()
    twin_copy(1).wait_send()
    for s in range(2):
        for n, ch in enumerate(chips):
            to_col(summed.at[s, ch], landed.at[s, ch], r_send.at[s, n], r_recv.at[s, ch], ch * 2 + core).wait_send()

    @pl.loop(1, 16)
    def _(i):
        to_col(tcol.at[me_c], tcol.at[me_c], tc_send.at[i], tc_recv.at[me_c], lax.rem(me_c + i, 16)).wait_send()
        to_row(trow.at[me_r], trow.at[me_r], tr_send.at[i], tr_recv.at[me_r], lax.rem(me_r + i, 16)).wait_send()

    store.wait()


def fast_call(table, dens):
    dma = pltpu.SemaphoreType.DMA
    return pl.pallas_call(
        kernel,
        out_shape=(
            jax.ShapeDtypeStruct((TILES, BLK, BLK), F32),
            jax.ShapeDtypeStruct((2, BLK, BLK), F32),
            jax.ShapeDtypeStruct((1, 1), F32),
        ),
        in_specs=[pl.BlockSpec(memory_space=pltpu.SMEM), pl.BlockSpec(memory_space=pl.ANY)],
        out_specs=(
            pl.BlockSpec(memory_space=pl.ANY),
            pl.BlockSpec(memory_space=pltpu.VMEM),
            pl.BlockSpec(memory_space=pltpu.SMEM),
        ),
        scratch_shapes=[
            pltpu.VMEM((TILES, BLK, BLK), F32),
            pltpu.VMEM((TILES + 1, BLK, BLK), BF),
            pltpu.VMEM((TILES + 1, BLK, BLK), BF),
            pltpu.VMEM((2, 8, PACK, BLK), BF),
            pltpu.VMEM((4, 4, PACK, BLK), BF),
            pltpu.VMEM((2, 8, PACK, BLK), BF),
            pltpu.VMEM((2, 8, PACK, BLK), BF),
            pltpu.VMEM((2, 8, PACK, BLK), BF),
            pltpu.VMEM((2, 8, PACK, BLK), BF),
            pltpu.VMEM((2, 8, PACK, BLK), BF),
            pltpu.VMEM((2, PACK, BLK), F32),
            pltpu.VMEM((32, BLK, BLK), BF),
            pltpu.VMEM((32, BLK, BLK), BF),
            pltpu.VMEM((32, BLK, BLK), BF),
            pltpu.VMEM((TILES, BLK, BLK), F32),
            pltpu.VMEM((TILES, BLK, BLK), F32),
            pltpu.VMEM((16, 8, BLK), F32),
            pltpu.VMEM((16, 8, BLK), F32),
            dma(()),
            dma((15,)), dma((2, 8)),
            dma((15,)), dma((4, 4)),
            dma((15,)), dma((2, 8)),
            dma((2,)), dma((2,)),
            dma((2, 7)), dma((2, 8)),
            dma((16,)), dma((16,)),
            dma((16,)), dma((16,)),
            dma(()),
        ],
        compiler_params=pltpu.CompilerParams(
            collective_id=0, has_side_effects=True, vmem_limit_bytes=40 * 1024 * 1024
        ),
    )(table, dens)


def index_table(own, tile_coords):
    rows, cols = own[:, 0], own[:, 1]
    column_class = (tile_coords[0, :, 0, 1] & 15).reshape(8, 2).T.reshape(16)
    match = (rows[:, None] & 15) == column_class[None, :]
    half = rows >> 8
    place = jnp.sum(jnp.where(match, jnp.arange(16, dtype=jnp.int32)[None, :], 0), axis=1)
    slots = jnp.arange(TILES, dtype=jnp.int32) - TILES
    hit = match[:, :, None] & (half[:, None, None] == jnp.arange(2, dtype=jnp.int32)[None, None, :])
    src = jnp.sum(jnp.where(hit, slots[:, None, None], 0), axis=0).reshape(32) + TILES
    band = cols >> 4
    gap = jnp.zeros((14,), jnp.int32)
    return jnp.concatenate([
        src,
        place * 2 + half, gap,
        (band & 15) * 2 + (band >> 4), gap,
        (rows == cols).astype(jnp.int32), gap,
    ])


def fast(density, tile_coords, own):
    out, special, trace = fast_call(index_table(own, tile_coords), density[0, 0])
    on_diag = own[:, 0] == own[:, 1]
    high = own[:, 0] >= NB // 2
    out = jnp.where(
        on_diag[:, None, None], jnp.where(high[:, None, None], special[1][None], special[0][None]), out
    )
    return out[None, None], trace[0, 0]


def pair_lookup(own_coords, targets, mirror_coords):
    own_rows = own_coords[:, 0]
    own_cols = own_coords[:, 1]
    target_row = targets[:, 0]
    target_col = targets[:, 1]
    first = (own_rows[None, :] == target_row[:, None]) & (target_row[:, None] >= 0)
    has_first = jnp.any(first, axis=1)
    left_slot = jnp.argmax(first.astype(jnp.int32), axis=1)
    inner = own_cols[left_slot]
    second = (mirror_coords[None, :, 0] == target_col[:, None]) & (
        mirror_coords[None, :, 1] == inner[:, None]
    )
    second = second & has_first[:, None]
    keep = jnp.any(second, axis=1)
    right_slot = jnp.argmax(second.astype(jnp.int32), axis=1)
    return (left_slot, right_slot, keep)


def scattered_product(left, mirror, left_slot, right_slot, keep):
    weight = keep.astype(F32)
    left_rows = jnp.take(left, left_slot, axis=0)
    right_rows = jnp.take(mirror, right_slot, axis=0)
    result = jnp.einsum("nik,njk->nij", left_rows, right_rows, preferred_element_type=F32)
    return lax.psum_scatter(
        (result * weight[:, None, None]).astype(BF), "col", scatter_dimension=0, tiled=True
    ).astype(F32)


def general(density, tile_coords, own_coords):
    own_tiles = density[0, 0]
    own_low = own_tiles.astype(BF)
    my_row = lax.axis_index("row")
    my_col = lax.axis_index("col")
    row_flat = jnp.take(tile_coords, my_row, axis=0).reshape(-1, 2)
    col_flat = jnp.take(tile_coords, my_col, axis=1).reshape(-1, 2)
    mirror = lax.all_gather(own_low, "row", axis=0, tiled=True)
    own_diag = own_coords[:, 0] == own_coords[:, 1]
    left_slot, right_slot, keep = pair_lookup(own_coords, row_flat, col_flat)
    square = scattered_product(own_low, mirror, left_slot, right_slot, keep)
    square_low = square.astype(BF)
    cube = scattered_product(square_low, mirror, left_slot, right_slot, keep)
    purified = 3.0 * square - 2.0 * cube
    total = lax.psum(
        jnp.sum(jnp.where(own_diag, jnp.einsum("nii->n", purified), 0.0)), ("row", "col")
    )
    return purified[None, None], total / (NB * BLK)


def per_device(density, tile_coords):
    own = lax.dynamic_slice(
        tile_coords, (lax.axis_index("row"), lax.axis_index("col"), 0, 0), (1, 1, TILES, 2)
    )[0, 0]
    offsets = (own[:, 1] - own[:, 0]) & (NB - 1)
    sums = (offsets[:, None] + offsets[None, :]) & (NB - 1)
    live = (offsets[:, None] != 0) & (offsets[None, :] != 0)
    triple = live[:, :, None] & (offsets != 0) & (sums[:, :, None] == offsets)
    return lax.cond(jnp.any(triple), general, fast, density, tile_coords, own)


def solution(mesh):
    return jax.shard_map(
        per_device,
        mesh=mesh,
        in_specs=(P("row", "col", None, None, None), P()),
        out_specs=(P("row", "col", None, None, None), P()),
        check_vma=False,
    )
```

```python
import jax
import jax.numpy as jnp
from jax import lax
from jax.experimental import pallas as pl
from jax.experimental.pallas import tpu as pltpu
from jax.sharding import PartitionSpec as P

NB = 512
BLK = 128
TILES = 18
PACK = BLK + 16
BF = jnp.bfloat16
F32 = jnp.float32
MESH = pl.DeviceIdType.MESH

CHIP_STEPS = ((0, 1), (0, 3), (1, 0), (0, 2), (1, 1), (1, 3), (1, 2))
RING_STEPS = (1, 3, 2)

SRC, DIDX, EIDX, KEY, TABLE = 0, 32, 64, 96, 128


def dot(a, b):
    return jnp.dot(a, b, preferred_element_type=F32)


def dot_t(a, b):
    return lax.dot_general(a, b, (((1,), (1,)), ((), ())), preferred_element_type=F32)


def each(n):
    return pl.loop(0, n, unroll=True)


def grids():
    row = lax.broadcasted_iota(jnp.int32, (BLK, BLK), 0)
    col = lax.broadcasted_iota(jnp.int32, (BLK, BLK), 1)
    return row, col


def pack(first, second):
    row, col = grids()
    body = jnp.where(row <= col, first, second)
    diag = jnp.sum(jnp.where(row == col, second, 0.0), axis=0, keepdims=True)
    return body, jnp.broadcast_to(diag, (PACK - BLK, BLK))


def unpack(body, diag):
    row, col = grids()
    turned = body.T
    first = jnp.where(row <= col, body, turned)
    second = jnp.where(row > col, body, jnp.where(row < col, turned, diag))
    return first, second


def fill_table(coords, table, me_c):
    def column_class(place):
        return coords[lax.rem(place, 8) * 2 + place // 8, 1, 0] & 15

    classes = [column_class(place) for place in range(16)]
    keys = []
    for t in range(TILES):
        i, j = coords[me_c, 0, t], coords[me_c, 1, t]
        residue, half = i & 15, i >> 8
        place = jnp.int32(0)
        for n in range(16):
            place = jnp.where(classes[n] == residue, n, place)
        table[DIDX + t] = place * 2 + half
        table[EIDX + t] = ((j >> 4) & 15) * 2 + (j >> 8)
        keys.append(place * 2 + half)
    for n in range(32):
        slot = jnp.int32(TILES)
        for t in range(TILES):
            slot = jnp.where(keys[t] == n, t, slot)
        table[SRC + n] = slot


def any_triple(coords, lanes, me_c):
    wide = (lanes[1:2] - lanes[0:1]) & (NB - 1)
    wide = jnp.where(wide == 0, -2, wide)
    offsets = [(coords[me_c, 1, t] - coords[me_c, 0, t]) & (NB - 1) for t in range(TILES)]
    found = jnp.zeros(wide.shape, jnp.int32)
    for s in range(TILES):
        for t in range(s, TILES):
            live = jnp.logical_and(offsets[s] != 0, offsets[t] != 0)
            both = jnp.where(live, (offsets[s] + offsets[t]) & (NB - 1), -1)
            found = found | (wide == both).astype(jnp.int32)
    return jnp.max(found)


def kernel(
    coords_hbm, dens_hbm, out_hbm, special, trace, flag,
    coords, table, lanes, dens, tiles, terms, dpack, epack, spack, mine, twins, summed, landed, sums,
    dfull, efull, sfull, square, outs, tcol, trow,
    load_sem, coord_sem, d_send, d_recv, e_send, e_recv, s_send, s_recv,
    x_send, x_recv, r_send, r_recv, tc_send, tc_recv, tr_send, tr_recv, out_sem,
):
    me_r = lax.axis_index("row")
    me_c = lax.axis_index("col")
    core = lax.rem(me_c, 2)
    other = 1 - core
    chip = me_c // 2
    zlo, y = chip // 4, lax.rem(chip, 4)
    zhi, x = me_r // 4, lax.rem(me_r, 4)
    twin = chip * 2 + other
    chips = [lax.rem(zlo + dz, 2) * 4 + lax.rem(y + dy, 4) for dz, dy in CHIP_STEPS]
    zs = [lax.rem(zhi + d, 4) for d in RING_STEPS]
    xs = [lax.rem(x + d, 4) for d in RING_STEPS]

    barrier = pltpu.get_barrier_semaphore()
    get_coords = pltpu.make_async_copy(coords_hbm.at[me_r], coords, coord_sem.at[0])
    get_lanes = pltpu.make_async_copy(coords_hbm.at[me_r, me_c], lanes, coord_sem.at[1])
    load = pltpu.make_async_copy(dens_hbm, dens, load_sem)
    get_coords.start()
    load.start()
    get_lanes.start()

    for i in range(1, 16):
        pl.semaphore_signal(barrier, inc=1, device_id={"row": lax.rem(me_r + i, 16)}, device_id_type=MESH)
    for i in range(1, 16):
        pl.semaphore_signal(barrier, inc=1, device_id={"col": lax.rem(me_c + i, 16)}, device_id_type=MESH)

    def to_col(src, dst, send, recv, c):
        return pltpu.make_async_remote_copy(
            src_ref=src, dst_ref=dst, send_sem=send, recv_sem=recv,
            device_id={"col": c}, device_id_type=MESH,
        )

    def to_row(src, dst, send, recv, r):
        return pltpu.make_async_remote_copy(
            src_ref=src, dst_ref=dst, send_sem=send, recv_sem=recv,
            device_id={"row": r}, device_id_type=MESH,
        )

    def spread_start(buf, send, recv):
        own = buf.at[core, chip]
        for n, ch in enumerate(chips):
            to_col(own, own, send.at[n], recv.at[core, chip], ch * 2 + core).start()
        to_col(own, own, send.at[7], recv.at[core, chip], twin).start()

    def spread_forward(buf, send, recv):
        for n, ch in enumerate(chips):
            part = buf.at[core, ch]
            copy = to_col(part, part, send.at[8 + n], recv.at[core, ch], twin)
            copy.wait_recv()
            copy.start()

    def spread_twin(buf, send, recv):
        for ch in [chip] + chips:
            part = buf.at[other, ch]
            to_col(part, part, send.at[0], recv.at[other, ch], twin).wait_recv()

    def spread_end(buf, send, recv):
        own = buf.at[core, chip]
        for n in range(15):
            to_col(own, own, send.at[n], recv.at[core, chip], twin).wait_send()

    def reduce_pack(skip_own, which):
        @each(8)
        def _(k):
            i0 = table[SRC + (which * 8 + k) * 2]
            i1 = table[SRC + (which * 8 + k) * 2 + 1]
            if skip_own:
                own = jnp.logical_and(which == core, k == chip)
                i0 = jnp.where(own, TILES, i0)
                i1 = jnp.where(own, TILES, i1)
            body, diag = pack(terms[i0].astype(F32), terms[i1].astype(F32))
            mine[which, k, 0:BLK] = body.astype(BF)
            mine[which, k, BLK:PACK] = diag.astype(BF)

    def twin_copy(s):
        return to_col(mine.at[other], twins.at[s], x_send.at[s], x_recv.at[s], twin)

    def reduce_send(s):
        twin_copy(s).wait_recv()

        @each(8)
        def _(k):
            summed[s, k] = (mine[core, k].astype(F32) + twins[s, k].astype(F32)).astype(BF)

        for n, ch in enumerate(chips):
            to_col(summed.at[s, ch], landed.at[s, chip], r_send.at[s, n], r_recv.at[s, chip], ch * 2 + core).start()

    def reduce_end(s):
        total = summed[s, chip].astype(F32)
        for n, ch in enumerate(chips):
            to_col(summed.at[s, ch], landed.at[s, ch], r_send.at[s, n], r_recv.at[s, ch], ch * 2 + core).wait_recv()
            total = total + landed[s, ch].astype(F32)
        sums[s] = total

    def expand(buf, which, k, full, at):
        first, second = unpack(buf[which, k, 0:BLK].astype(F32), buf[which, k, BLK:BLK + 1].astype(F32))
        full[at] = first.astype(BF)
        full[at + 1] = second.astype(BF)

    def expand_half(buf, which, full):
        @each(8)
        def _(k):
            expand(buf, which, k, full, (which * 8 + k) * 2)

    def fold(v):
        return jnp.sum(v.reshape(BLK // 8, 8, BLK), axis=0)

    get_coords.wait()
    fill_table(coords, table, me_c)
    load.wait()

    @each(TILES)
    def _(t):
        tiles[t] = dens[t].astype(BF)

    zero = jnp.zeros((BLK, BLK), BF)
    tiles[TILES] = zero
    terms[TILES] = zero
    my_pos = (core * 8 + chip) * 2
    own0 = table[SRC + my_pos]
    own1 = table[SRC + my_pos + 1]
    body, diag = pack(tiles[own0].astype(F32), tiles[own1].astype(F32))
    body, diag = body.astype(BF), diag.astype(BF)
    dpack[core, chip, 0:BLK] = body
    dpack[core, chip, BLK:PACK] = diag
    epack[zhi, x, 0:BLK] = body
    epack[zhi, x, BLK:PACK] = diag

    @each(TILES)
    def _(t):
        b = tiles[t]
        terms[t] = dot_t(b, b).astype(BF)

    reduce_pack(False, other)

    pl.semaphore_wait(barrier, 30)

    def along_z(n):
        own = epack.at[zhi, x]
        return to_row(own, own, e_send.at[n], e_recv.at[zhi, x], zs[n] * 4 + x)

    def along_x(z, m, n):
        part = epack.at[z, x]
        return to_row(part, part, e_send.at[m], e_recv.at[z, x], zhi * 4 + xs[n])

    def arrived(z, k):
        part = epack.at[z, k]
        to_row(part, part, e_send.at[0], e_recv.at[z, k], me_r).wait_recv()

    for n in range(3):
        along_z(n).start()
    twin_copy(0).start()
    for n in range(3):
        along_x(zhi, 3 + n, n).start()
    reduce_pack(False, core)
    reduce_send(0)
    spread_start(dpack, d_send, d_recv)

    for n in range(3):
        arrived(zs[n], x)
        for m in range(3):
            along_x(zs[n], 6 + 3 * n + m, m).start()

    get_lanes.wait()
    flag[0, 0] = any_triple(coords, lanes, me_c)
    spread_forward(dpack, d_send, d_recv)

    reduce_end(0)
    spack[core, chip] = sums[0].astype(BF)
    spread_start(spack, s_send, s_recv)

    acc = jnp.zeros((8, BLK), F32)
    row, col = grids()
    for h, s in enumerate(unpack(sums[0, 0:BLK], sums[0, BLK:BLK + 1])):
        d = tiles[own0 if h == 0 else own1]
        wide = d.astype(F32)
        low = s.astype(BF)
        rest = s - dot(d, d)
        special[h] = 3.0 * s - 2.0 * (dot(d, rest.astype(BF)) + dot(low, d))
        acc = acc + fold(jnp.where(row == col, 3.0 * s, 0.0) - wide * (4.0 * rest + 2.0 * s))
    tcol[me_c] = acc
    for i in range(1, 16):
        to_col(tcol.at[me_c], tcol.at[me_c], tc_send.at[i], tc_recv.at[me_c], lax.rem(me_c + i, 16)).start()

    expand_half(dpack, core, dfull)
    spread_twin(dpack, d_send, d_recv)
    expand_half(dpack, other, dfull)

    @each(TILES)
    def _(t):
        square[t] = dot(dfull[table[DIDX + t]], tiles[t])

    for n in range(3):
        arrived(zhi, xs[n])
    for m in range(3):
        for n in range(3):
            arrived(zs[m], xs[n])

    @each(16)
    def _(k):
        expand(epack, k // 4, lax.rem(k, 4), efull, k * 2)

    twin_copy(0).wait_send()

    @each(TILES)
    def _(t):
        b = tiles[t]
        f = dot(b, efull[table[EIDX + t]])
        square[t] = square[t] + f
        terms[t] = dot_t(f.astype(BF), b).astype(BF)

    reduce_pack(True, other)
    twin_copy(1).start()
    reduce_pack(True, core)

    for i in range(1, 16):
        c = lax.rem(me_c + i, 16)
        to_col(tcol.at[c], tcol.at[c], tc_send.at[i], tc_recv.at[c], c).wait_recv()
    trow[me_r] = jnp.sum(tcol[...], axis=0)
    for i in range(1, 16):
        to_row(trow.at[me_r], trow.at[me_r], tr_send.at[i], tr_recv.at[me_r], lax.rem(me_r + i, 16)).start()

    reduce_send(1)
    spread_forward(spack, s_send, s_recv)

    @each(TILES)
    def _(t):
        s = square[t]
        outs[t] = 3.0 * s - 2.0 * dot(s.astype(BF), efull[table[EIDX + t]])

    expand_half(spack, core, sfull)
    spread_twin(spack, s_send, s_recv)
    expand_half(spack, other, sfull)

    @each(TILES)
    def _(t):
        outs[t] = outs[t] - 2.0 * dot(sfull[table[DIDX + t]], tiles[t])

    store = pltpu.make_async_copy(outs, out_hbm, out_sem)
    store.start()

    reduce_end(1)
    for h, q in enumerate(unpack(sums[1, 0:BLK], sums[1, BLK:BLK + 1])):
        special[h] = special[h] - 2.0 * q

    for i in range(1, 16):
        r = lax.rem(me_r + i, 16)
        to_row(trow.at[r], trow.at[r], tr_send.at[i], tr_recv.at[r], r).wait_recv()
    trace[0, 0] = jnp.sum(trow[...]) / (NB * BLK)

    spread_end(dpack, d_send, d_recv)
    spread_end(spack, s_send, s_recv)
    own = epack.at[zhi, x]
    for n in range(15):
        to_row(own, own, e_send.at[n], e_recv.at[zhi, x], me_r).wait_send()
    twin_copy(1).wait_send()
    for s in range(2):
        for n, ch in enumerate(chips):
            to_col(summed.at[s, ch], landed.at[s, ch], r_send.at[s, n], r_recv.at[s, ch], ch * 2 + core).wait_send()
    for i in range(1, 16):
        to_col(tcol.at[me_c], tcol.at[me_c], tc_send.at[i], tc_recv.at[me_c], lax.rem(me_c + i, 16)).wait_send()
        to_row(trow.at[me_r], trow.at[me_r], tr_send.at[i], tr_recv.at[me_r], lax.rem(me_r + i, 16)).wait_send()
    store.wait()


def fast_call(coords, dens):
    dma = pltpu.SemaphoreType.DMA
    pair = (2, 8, PACK, BLK)
    return pl.pallas_call(
        kernel,
        out_shape=(
            jax.ShapeDtypeStruct((TILES, BLK, BLK), F32),
            jax.ShapeDtypeStruct((2, BLK, BLK), F32),
            jax.ShapeDtypeStruct((1, 1), F32),
            jax.ShapeDtypeStruct((1, 1), jnp.int32),
        ),
        in_specs=[pl.BlockSpec(memory_space=pl.ANY), pl.BlockSpec(memory_space=pl.ANY)],
        out_specs=(
            pl.BlockSpec(memory_space=pl.ANY),
            pl.BlockSpec(memory_space=pltpu.VMEM),
            pl.BlockSpec(memory_space=pltpu.SMEM),
            pl.BlockSpec(memory_space=pltpu.SMEM),
        ),
        scratch_shapes=[
            pltpu.SMEM((16, 2, TILES), jnp.int32),
            pltpu.SMEM((TABLE,), jnp.int32),
            pltpu.VMEM((2, TILES), jnp.int32),
            pltpu.VMEM((TILES, BLK, BLK), F32),
            pltpu.VMEM((TILES + 1, BLK, BLK), BF),
            pltpu.VMEM((TILES + 1, BLK, BLK), BF),
            pltpu.VMEM(pair, BF),
            pltpu.VMEM((4, 4, PACK, BLK), BF),
            pltpu.VMEM(pair, BF),
            pltpu.VMEM(pair, BF),
            pltpu.VMEM(pair, BF),
            pltpu.VMEM(pair, BF),
            pltpu.VMEM(pair, BF),
            pltpu.VMEM((2, PACK, BLK), F32),
            pltpu.VMEM((32, BLK, BLK), BF),
            pltpu.VMEM((32, BLK, BLK), BF),
            pltpu.VMEM((32, BLK, BLK), BF),
            pltpu.VMEM((TILES, BLK, BLK), F32),
            pltpu.VMEM((TILES, BLK, BLK), F32),
            pltpu.VMEM((16, 8, BLK), F32),
            pltpu.VMEM((16, 8, BLK), F32),
            dma(()), dma((2,)),
            dma((15,)), dma((2, 8)),
            dma((15,)), dma((4, 4)),
            dma((15,)), dma((2, 8)),
            dma((2,)), dma((2,)),
            dma((2, 7)), dma((2, 8)),
            dma((16,)), dma((16,)),
            dma((16,)), dma((16,)),
            dma(()),
        ],
        compiler_params=pltpu.CompilerParams(
            collective_id=0, has_side_effects=True, vmem_limit_bytes=40 * 1024 * 1024
        ),
    )(coords, dens)


def pair_lookup(own_coords, targets, mirror_coords):
    own_rows = own_coords[:, 0]
    own_cols = own_coords[:, 1]
    target_row = targets[:, 0]
    target_col = targets[:, 1]
    first = own_rows[None, :] == target_row[:, None]
    has_first = jnp.any(first, axis=1)
    left_slot = jnp.argmax(first.astype(jnp.int32), axis=1)
    inner = own_cols[left_slot]
    second = (mirror_coords[None, :, 0] == target_col[:, None]) & (
        mirror_coords[None, :, 1] == inner[:, None]
    )
    second = second & has_first[:, None]
    keep = jnp.any(second, axis=1)
    right_slot = jnp.argmax(second.astype(jnp.int32), axis=1)
    return (left_slot, right_slot, keep)


def to_all(value, axis):
    return lax.all_to_all(jnp.broadcast_to(value[None], (16,) + value.shape), axis, 0, 0)


def scattered_product(left, mirror, left_slot, right_slot, keep):
    weight = keep.astype(F32)
    left_rows = jnp.take(left, left_slot, axis=0)
    right_rows = jnp.take(mirror, right_slot, axis=0)
    result = jnp.einsum("nik,njk->nij", left_rows, right_rows, preferred_element_type=F32)
    result = (result * weight[:, None, None]).astype(BF).reshape(16, TILES, BLK, BLK)
    return jnp.sum(lax.all_to_all(result, "col", 0, 0).astype(F32), axis=0)


def general(density, tile_coords):
    own_tiles = density[0, 0]
    own_low = own_tiles.astype(BF)
    my_row = lax.axis_index("row")
    my_col = lax.axis_index("col")
    row_table = jnp.take(tile_coords, my_row, axis=0)
    own_coords = jnp.take(row_table, my_col, axis=0)
    row_flat = row_table.reshape(-1, 2)
    col_flat = jnp.take(tile_coords, my_col, axis=1).reshape(-1, 2)
    mirror = to_all(own_low, "row").reshape(-1, BLK, BLK)
    own_diag = own_coords[:, 0] == own_coords[:, 1]
    left_slot, right_slot, keep = pair_lookup(own_coords, row_flat, col_flat)
    square = scattered_product(own_low, mirror, left_slot, right_slot, keep)
    square_low = square.astype(BF)
    cube = scattered_product(square_low, mirror, left_slot, right_slot, keep)
    purified = 3.0 * square - 2.0 * cube
    total = jnp.sum(jnp.where(own_diag, jnp.einsum("nii->n", purified), 0.0))
    total = jnp.sum(to_all(jnp.sum(to_all(total, "col")), "row"))
    return purified, total / (NB * BLK)


def per_device(density, tile_coords):
    out, special, trace, flag = fast_call(tile_coords.transpose(0, 1, 3, 2), density[0, 0])
    own = lax.dynamic_slice(
        tile_coords, (lax.axis_index("row"), lax.axis_index("col"), 0, 0), (1, 1, TILES, 2)
    )[0, 0]
    on_diag = own[:, 0] == own[:, 1]
    high = own[:, 0] >= NB // 2
    out = jnp.where(
        on_diag[:, None, None], jnp.where(high[:, None, None], special[1][None], special[0][None]), out
    )
    out, mean_diagonal = lax.cond(
        flag[0, 0] > 0,
        lambda out, trace: general(density, tile_coords),
        lambda out, trace: (out, trace),
        out, trace[0, 0],
    )
    return out[None, None], mean_diagonal


def solution(mesh):
    return jax.shard_map(
        per_device,
        mesh=mesh,
        in_specs=(P("row", "col", None, None, None), P()),
        out_specs=(P("row", "col", None, None, None), P()),
        check_vma=False,
    )
```

```python
import jax
import jax.numpy as jnp
from jax import lax
from jax.experimental import pallas as pl
from jax.experimental.pallas import tpu as pltpu
from jax.sharding import PartitionSpec as P

NB = 512
BLK = 128
TILES = 18
PACK = BLK + 16
BF = jnp.bfloat16
F32 = jnp.float32
MESH = pl.DeviceIdType.MESH

CHIP_STEPS = ((0, 0), (0, 1), (0, 3), (1, 0), (0, 2), (1, 1), (1, 3), (1, 2))
CHIP_BACK = tuple(CHIP_STEPS.index((-dz % 2, -dy % 4)) for dz, dy in CHIP_STEPS)
RING = (0, 1, 3, 2)
RING_BACK = tuple(RING.index(-d % 4) for d in RING)

SRC, DIDX, EIDX, TABLE = 0, 32, 64, 96


def dot(a, b):
    return jnp.dot(a, b, preferred_element_type=F32)


def dot_t(a, b):
    return lax.dot_general(a, b, (((1,), (1,)), ((), ())), preferred_element_type=F32)


def each(lo, hi):
    return pl.loop(lo, hi, unroll=True)


def grids():
    row = lax.broadcasted_iota(jnp.int32, (BLK, BLK), 0)
    col = lax.broadcasted_iota(jnp.int32, (BLK, BLK), 1)
    return row, col


def pack(first, second):
    row, col = grids()
    body = jnp.where(row <= col, first, second)
    diag = jnp.sum(jnp.where(row == col, second, 0.0), axis=0, keepdims=True)
    return body, jnp.broadcast_to(diag, (PACK - BLK, BLK))


def unpack(body, diag):
    row, col = grids()
    turned = body.T
    first = jnp.where(row <= col, body, turned)
    second = jnp.where(row > col, body, jnp.where(row < col, turned, diag))
    return first, second


def fill_table(coords, table, which, me_r, me_c, places):
    classes = [coords[c, 1, 0] & 15 for c in places]
    zhi, x = me_r // 4, lax.rem(me_r, 4)
    keys = []
    for t in range(TILES):
        i, j = coords[me_c, 0, t], coords[me_c, 1, t]
        residue, half = i & 15, i >> 8
        place = jnp.int32(0)
        for n in range(16):
            place = jnp.where(classes[n] == residue, n, place)
        key = place * 2 + half
        keys.append(key)
        table[DIDX + t] = key
        dz, dx = ((j >> 6) - zhi) & 3, ((j >> 4) - x) & 3
        table[EIDX + t] = ((dx ^ (dx >> 1)) * 4 + (dz ^ (dz >> 1))) * 2 + (j >> 8)
        which[t] = jnp.where(i == j, 1 + half, 0)
    for n in range(32):
        slot = jnp.int32(TILES)
        for t in range(TILES):
            slot = jnp.where(keys[t] == n, t, slot)
        table[SRC + n] = slot


def diagonal_slots(coords, me_c):
    first, second = jnp.int32(0), jnp.int32(0)
    for t in range(TILES):
        i, j = coords[me_c, 0, t], coords[me_c, 1, t]
        first = jnp.where(jnp.logical_and(i == j, i < NB // 2), t, first)
        second = jnp.where(jnp.logical_and(i == j, i >= NB // 2), t, second)
    return first, second


def any_triple(coords, lanes, me_c):
    wide = (lanes[1:2] - lanes[0:1]) & (NB - 1)
    wide = jnp.where(wide == 0, -2, wide)
    offsets = [(coords[me_c, 1, t] - coords[me_c, 0, t]) & (NB - 1) for t in range(TILES)]
    found = jnp.zeros(wide.shape, jnp.int32)
    for s in range(TILES):
        for t in range(s, TILES):
            live = jnp.logical_and(offsets[s] != 0, offsets[t] != 0)
            both = jnp.where(live, (offsets[s] + offsets[t]) & (NB - 1), -1)
            found = found | (wide == both).astype(jnp.int32)
    return jnp.max(found)


def kernel(
    coords_hbm, dens_hbm, out_hbm, special, trace, flag, which,
    coords, table, lanes, dens, tiles, terms, dpack, epack, spack, mine, twins, summed, landed, sums,
    dfull, efull, sfull, square, outs, ttwin, tcol, tz, tx,
    load_sem, d_send, d_recv, e_send, ez_recv, ex_recv, s_send, s_recv,
    x_send, x_recv, r_send, r_recv, t_send, t_recv, out_sem,
):
    me_r = lax.axis_index("row")
    me_c = lax.axis_index("col")
    core = lax.rem(me_c, 2)
    chip = me_c // 2
    zlo, y = chip // 4, lax.rem(chip, 4)
    zhi, x = me_r // 4, lax.rem(me_r, 4)
    chips = [lax.rem(zlo + dz, 2) * 4 + lax.rem(y + dy, 4) for dz, dy in CHIP_STEPS]
    same = [ch * 2 + core for ch in chips]
    places = same + [ch * 2 + 1 - core for ch in chips]
    twin = places[8]
    zs = [lax.rem(zhi + d, 4) * 4 + x for d in RING]
    xs = [zhi * 4 + lax.rem(x + d, 4) for d in RING]

    barrier = pltpu.get_barrier_semaphore()
    get_coords = pltpu.make_async_copy(coords_hbm.at[me_r], coords, load_sem.at[0])
    load = pltpu.make_async_copy(dens_hbm, dens, load_sem.at[1])
    get_lanes = pltpu.make_async_copy(coords_hbm.at[me_r, me_c], lanes, load_sem.at[2])
    get_coords.start()
    load.start()
    for b in (3, 2, 1):
        pl.semaphore_signal(barrier, inc=1, device_id={"row": zs[b]}, device_id_type=MESH)
    for k in range(7, 0, -1):
        pl.semaphore_signal(barrier, inc=1, device_id={"col": same[k]}, device_id_type=MESH)
    for a in (3, 2, 1):
        pl.semaphore_signal(barrier, inc=1, device_id={"row": xs[a]}, device_id_type=MESH)
    pl.semaphore_signal(barrier, inc=1, device_id={"col": twin}, device_id_type=MESH)
    get_lanes.start()

    def to_col(src, dst, send, recv, c):
        return pltpu.make_async_remote_copy(
            src_ref=src, dst_ref=dst, send_sem=send, recv_sem=recv,
            device_id={"col": c}, device_id_type=MESH,
        )

    def to_row(src, dst, send, recv, r):
        return pltpu.make_async_remote_copy(
            src_ref=src, dst_ref=dst, send_sem=send, recv_sem=recv,
            device_id={"row": r}, device_id_type=MESH,
        )

    def spread_start(buf, send, recv):
        for k in range(1, 8):
            to_col(buf.at[0, 0], buf.at[0, CHIP_BACK[k]], send.at[0], recv.at[0], same[k]).start()

    def spread_seven(buf, send, recv):
        part = buf.at[0, 1:8]
        return to_col(part, part, send.at[0], recv.at[0], twin)

    def spread_twin(buf, send, recv):
        return to_col(buf.at[0], buf.at[1], send.at[1], recv.at[1], twin)

    def reduce_pack(rc, first):
        @each(first, 8)
        def _(k):
            n = rc * 8 + k
            body, diag = pack(terms[table[SRC + n * 2]].astype(F32), terms[table[SRC + n * 2 + 1]].astype(F32))
            mine[rc, k, 0:BLK] = body.astype(BF)
            mine[rc, k, BLK:PACK] = diag.astype(BF)

    def twin_copy(s):
        return to_col(mine.at[1], twins.at[s], x_send.at[s], x_recv.at[s], twin)

    def reduce_send(s):
        twin_copy(s).wait_recv()
        for k in range(7, -1, -1):
            summed[s, k] = (mine[0, k].astype(F32) + twins[s, k].astype(F32)).astype(BF)
            if k:
                to_col(summed.at[s, k], landed.at[s, CHIP_BACK[k]], r_send.at[s], r_recv.at[s], same[k]).start()

    def reduce_seven(s):
        return to_col(summed.at[s, 1:8], landed.at[s, 1:8], r_send.at[s], r_recv.at[s], twin)

    def reduce_end(s):
        reduce_seven(s).wait_recv()
        total = summed[s, 0].astype(F32)
        for k in range(1, 8):
            total = total + landed[s, k].astype(F32)
        sums[s] = total

    def expand(buf, n, m, full, at):
        first, second = unpack(buf[n, m, 0:BLK].astype(F32), buf[n, m, BLK:BLK + 1].astype(F32))
        full[at] = first.astype(BF)
        full[at + 1] = second.astype(BF)

    def expand_half(buf, rc, full):
        @each(0, 8)
        def _(k):
            expand(buf, rc, k, full, (rc * 8 + k) * 2)

    def fold(v):
        return jnp.sum(v.reshape(BLK // 8, 8, BLK), axis=0)

    get_coords.wait()
    own0, own1 = diagonal_slots(coords, me_c)
    load.wait()

    @each(0, TILES)
    def _(t):
        tiles[t] = dens[t].astype(BF)

    zero = jnp.zeros((BLK, BLK), BF)
    tiles[TILES] = zero
    terms[TILES] = zero
    body, diag = pack(tiles[own0].astype(F32), tiles[own1].astype(F32))
    body, diag = body.astype(BF), diag.astype(BF)
    dpack[0, 0, 0:BLK] = body
    dpack[0, 0, BLK:PACK] = diag
    epack[0, 0, 0:BLK] = body
    epack[0, 0, BLK:PACK] = diag

    pl.semaphore_wait(barrier, 14)
    for b in (3, 1, 2):
        to_row(epack.at[0, 0], epack.at[0, RING_BACK[b]], e_send.at[0], ez_recv.at[b // 3], zs[b]).start()

    def along_x(lo, hi, n):
        for a in (3, 1, 2):
            to_row(
                epack.at[0, lo:hi], epack.at[RING_BACK[a], lo:hi], e_send.at[1 + n], ex_recv.at[n], xs[a]
            ).start()

    def ring_wait(part, sem):
        return to_row(part, part, e_send.at[0], sem, me_r)

    along_x(0, 1, 0)

    fill_table(coords, table, which, me_r, me_c, places)

    @each(0, TILES)
    def _(t):
        b = tiles[t]
        terms[t] = dot_t(b, b).astype(BF)

    reduce_pack(1, 0)
    twin_copy(0).start()
    reduce_pack(0, 0)

    ring_wait(epack.at[0, 1:3], ez_recv.at[0]).wait_recv()
    along_x(1, 3, 0)
    reduce_send(0)
    ring_wait(epack.at[0, 3], ez_recv.at[1]).wait_recv()
    along_x(3, 4, 1)
    spread_start(dpack, d_send, d_recv)

    get_lanes.wait()
    flag[0, 0] = any_triple(coords, lanes, me_c)

    reduce_end(0)
    spack[0, 0] = sums[0].astype(BF)
    spread_start(spack, s_send, s_recv)

    acc = jnp.zeros((8, BLK), F32)
    row, col = grids()
    for h, s in enumerate(unpack(sums[0, 0:BLK], sums[0, BLK:BLK + 1])):
        d = tiles[own0 if h == 0 else own1]
        wide = d.astype(F32)
        low = s.astype(BF)
        rest = s - dot(d, d)
        special[h] = 3.0 * s - 2.0 * (dot(d, rest.astype(BF)) + dot(low, d))
        acc = acc + fold(jnp.where(row == col, 3.0 * s, 0.0) - wide * (4.0 * rest + 2.0 * s))
    ttwin[0] = acc
    trace_twin = to_col(ttwin.at[0], ttwin.at[1], t_send.at[0], t_recv.at[0], twin)
    trace_twin.start()

    spread_seven(dpack, d_send, d_recv).wait_recv()
    spread_twin(dpack, d_send, d_recv).start()
    expand_half(dpack, 0, dfull)

    trace_twin.wait_recv()
    tcol[0] = ttwin[0] + ttwin[1]
    for k in range(1, 8):
        to_col(tcol.at[0], tcol.at[CHIP_BACK[k]], t_send.at[1], t_recv.at[1], same[k]).start()

    spread_twin(dpack, d_send, d_recv).wait_recv()
    expand_half(dpack, 1, dfull)

    @each(0, TILES)
    def _(t):
        square[t] = dot(dfull[table[DIDX + t]], tiles[t])

    for b in range(4):
        expand(epack, 0, b, efull, b * 2)
    ring_wait(epack.at[1:4, 0:3], ex_recv.at[0]).wait_recv()
    for a in range(1, 4):
        for b in range(3):
            expand(epack, a, b, efull, (a * 4 + b) * 2)
    twin_copy(0).wait_send()
    ring_wait(epack.at[1:4, 3], ex_recv.at[1]).wait_recv()
    for a in range(1, 4):
        expand(epack, a, 3, efull, (a * 4 + 3) * 2)

    @each(0, TILES)
    def _(t):
        b = tiles[t]
        f = dot(b, efull[table[EIDX + t]])
        square[t] = square[t] + f
        terms[t] = dot_t(f.astype(BF), b).astype(BF)

    reduce_pack(1, 0)
    twin_copy(1).start()
    reduce_pack(0, 1)
    mine[0, 0] = jnp.zeros((PACK, BLK), BF)

    tcol_seven = to_col(tcol.at[1:8], tcol.at[1:8], t_send.at[1], t_recv.at[1], twin)
    tcol_seven.wait_recv()
    tz[0] = jnp.sum(tcol[...], axis=0)
    for b in (3, 1, 2):
        to_row(tz.at[0], tz.at[RING_BACK[b]], t_send.at[2], t_recv.at[2], zs[b]).start()

    reduce_send(1)

    @each(0, TILES)
    def _(t):
        s = square[t]
        outs[t] = 3.0 * s - 2.0 * dot(s.astype(BF), efull[table[EIDX + t]])

    spread_seven(spack, s_send, s_recv).wait_recv()
    spread_twin(spack, s_send, s_recv).start()
    expand_half(spack, 0, sfull)
    spread_twin(spack, s_send, s_recv).wait_recv()
    expand_half(spack, 1, sfull)

    @each(0, TILES)
    def _(t):
        outs[t] = outs[t] - 2.0 * dot(sfull[table[DIDX + t]], tiles[t])

    store = pltpu.make_async_copy(outs, out_hbm, out_sem)
    store.start()

    tz_three = to_row(tz.at[1:4], tz.at[1:4], t_send.at[2], t_recv.at[2], me_r)
    tz_three.wait_recv()
    tx[0] = jnp.sum(tz[...], axis=0)
    for a in (3, 1, 2):
        to_row(tx.at[0], tx.at[RING_BACK[a]], t_send.at[3], t_recv.at[3], xs[a]).start()

    reduce_end(1)
    for h, q in enumerate(unpack(sums[1, 0:BLK], sums[1, BLK:BLK + 1])):
        special[h] = special[h] - 2.0 * q

    for buf, send, recv in ((dpack, d_send, d_recv), (spack, s_send, s_recv)):
        spread_seven(buf, send, recv).wait_send()
        spread_twin(buf, send, recv).wait_send()
    ring_wait(epack.at[0, 1:4], ez_recv.at[0]).wait_send()
    part = epack.at[1:4, 0:3]
    to_row(part, part, e_send.at[1], ex_recv.at[0], me_r).wait_send()
    part = epack.at[1:4, 3]
    to_row(part, part, e_send.at[2], ex_recv.at[1], me_r).wait_send()
    twin_copy(1).wait_send()
    reduce_seven(0).wait_send()
    reduce_seven(1).wait_send()
    trace_twin.wait_send()
    tcol_seven.wait_send()
    tz_three.wait_send()

    tx_three = to_row(tx.at[1:4], tx.at[1:4], t_send.at[3], t_recv.at[3], me_r)
    tx_three.wait_recv()
    trace[0, 0] = jnp.sum(tx[...]) / (NB * BLK)
    tx_three.wait_send()
    store.wait()


def fast_call(coords, dens):
    dma = pltpu.SemaphoreType.DMA
    pair = (2, 8, PACK, BLK)
    smem = pl.BlockSpec(memory_space=pltpu.SMEM)
    return pl.pallas_call(
        kernel,
        out_shape=(
            jax.ShapeDtypeStruct((TILES, BLK, BLK), F32),
            jax.ShapeDtypeStruct((2, BLK, BLK), F32),
            jax.ShapeDtypeStruct((1, 1), F32),
            jax.ShapeDtypeStruct((1, 1), jnp.int32),
            jax.ShapeDtypeStruct((TILES,), jnp.int32),
        ),
        in_specs=[pl.BlockSpec(memory_space=pl.ANY), pl.BlockSpec(memory_space=pl.ANY)],
        out_specs=(
            pl.BlockSpec(memory_space=pl.ANY), pl.BlockSpec(memory_space=pltpu.VMEM), smem, smem, smem,
        ),
        scratch_shapes=[
            pltpu.SMEM((16, 2, TILES), jnp.int32),
            pltpu.SMEM((TABLE,), jnp.int32),
            pltpu.VMEM((2, TILES), jnp.int32),
            pltpu.VMEM((TILES, BLK, BLK), F32),
            pltpu.VMEM((TILES + 1, BLK, BLK), BF),
            pltpu.VMEM((TILES + 1, BLK, BLK), BF),
            pltpu.VMEM(pair, BF),
            pltpu.VMEM((4, 4, PACK, BLK), BF),
            pltpu.VMEM(pair, BF),
            pltpu.VMEM(pair, BF),
            pltpu.VMEM(pair, BF),
            pltpu.VMEM(pair, BF),
            pltpu.VMEM(pair, BF),
            pltpu.VMEM((2, PACK, BLK), F32),
            pltpu.VMEM((32, BLK, BLK), BF),
            pltpu.VMEM((32, BLK, BLK), BF),
            pltpu.VMEM((32, BLK, BLK), BF),
            pltpu.VMEM((TILES, BLK, BLK), F32),
            pltpu.VMEM((TILES, BLK, BLK), F32),
            pltpu.VMEM((2, 8, BLK), F32),
            pltpu.VMEM((8, 8, BLK), F32),
            pltpu.VMEM((4, 8, BLK), F32),
            pltpu.VMEM((4, 8, BLK), F32),
            dma((3,)),
            dma((2,)), dma((2,)),
            dma((3,)), dma((2,)), dma((2,)),
            dma((2,)), dma((2,)),
            dma((2,)), dma((2,)),
            dma((2,)), dma((2,)),
            dma((4,)), dma((4,)),
            dma(()),
        ],
        compiler_params=pltpu.CompilerParams(
            collective_id=0, has_side_effects=True, vmem_limit_bytes=40 * 1024 * 1024
        ),
    )(coords, dens)


def pair_lookup(own_coords, targets, mirror_coords):
    own_rows = own_coords[:, 0]
    own_cols = own_coords[:, 1]
    target_row = targets[:, 0]
    target_col = targets[:, 1]
    first = own_rows[None, :] == target_row[:, None]
    has_first = jnp.any(first, axis=1)
    left_slot = jnp.argmax(first.astype(jnp.int32), axis=1)
    inner = own_cols[left_slot]
    second = (mirror_coords[None, :, 0] == target_col[:, None]) & (
        mirror_coords[None, :, 1] == inner[:, None]
    )
    second = second & has_first[:, None]
    keep = jnp.any(second, axis=1)
    right_slot = jnp.argmax(second.astype(jnp.int32), axis=1)
    return (left_slot, right_slot, keep)


def to_all(value, axis):
    return lax.all_to_all(jnp.broadcast_to(value[None], (16,) + value.shape), axis, 0, 0)


def scattered_product(left, mirror, left_slot, right_slot, keep):
    weight = keep.astype(F32)
    left_rows = jnp.take(left, left_slot, axis=0)
    right_rows = jnp.take(mirror, right_slot, axis=0)
    result = jnp.einsum("nik,njk->nij", left_rows, right_rows, preferred_element_type=F32)
    result = (result * weight[:, None, None]).astype(BF).reshape(16, TILES, BLK, BLK)
    return jnp.sum(lax.all_to_all(result, "col", 0, 0).astype(F32), axis=0)


def general(density, tile_coords):
    own_tiles = density[0, 0]
    own_low = own_tiles.astype(BF)
    my_row = lax.axis_index("row")
    my_col = lax.axis_index("col")
    row_table = jnp.take(tile_coords, my_row, axis=0)
    own_coords = jnp.take(row_table, my_col, axis=0)
    row_flat = row_table.reshape(-1, 2)
    col_flat = jnp.take(tile_coords, my_col, axis=1).reshape(-1, 2)
    mirror = to_all(own_low, "row").reshape(-1, BLK, BLK)
    own_diag = own_coords[:, 0] == own_coords[:, 1]
    left_slot, right_slot, keep = pair_lookup(own_coords, row_flat, col_flat)
    square = scattered_product(own_low, mirror, left_slot, right_slot, keep)
    square_low = square.astype(BF)
    cube = scattered_product(square_low, mirror, left_slot, right_slot, keep)
    purified = 3.0 * square - 2.0 * cube
    total = jnp.sum(jnp.where(own_diag, jnp.einsum("nii->n", purified), 0.0))
    total = jnp.sum(to_all(jnp.sum(to_all(total, "col")), "row"))
    return purified, total / (NB * BLK)


def per_device(density, tile_coords):
    out, special, trace, flag, which = fast_call(tile_coords.transpose(0, 1, 3, 2), density[0, 0])
    which = which[:, None, None]
    out = jnp.where(which == 0, out, jnp.where(which == 1, special[0][None], special[1][None]))
    out, mean_diagonal = lax.cond(
        flag[0, 0] > 0,
        lambda out, trace: general(density, tile_coords),
        lambda out, trace: (out, trace),
        out, trace[0, 0],
    )
    return out[None, None], mean_diagonal


def solution(mesh):
    return jax.shard_map(
        per_device,
        mesh=mesh,
        in_specs=(P("row", "col", None, None, None), P()),
        out_specs=(P("row", "col", None, None, None), P()),
        check_vma=False,
    )
```

```python
import jax
import jax.numpy as jnp
from jax import lax
from jax.experimental import pallas as pl
from jax.experimental.pallas import tpu as pltpu
from jax.sharding import PartitionSpec as P

NB = 512
BLK = 128
TILES = 18
PACK = BLK + 16
BF = jnp.bfloat16
F32 = jnp.float32
MESH = pl.DeviceIdType.MESH

CHIP_STEPS = ((0, 0), (0, 1), (0, 3), (1, 0), (0, 2), (1, 1), (1, 3), (1, 2))
CHIP_BACK = tuple(CHIP_STEPS.index((-dz % 2, -dy % 4)) for dz, dy in CHIP_STEPS)
RING = (0, 1, 3, 2)
RING_BACK = tuple(RING.index(-d % 4) for d in RING)

SRC, DIDX, EIDX, TABLE = 0, 32, 64, 96


def dot(a, b):
    return jnp.dot(a, b, preferred_element_type=F32)


def dot_t(a, b):
    return lax.dot_general(a, b, (((1,), (1,)), ((), ())), preferred_element_type=F32)


def each(lo, hi):
    return pl.loop(lo, hi, unroll=True)


def grids():
    row = lax.broadcasted_iota(jnp.int32, (BLK, BLK), 0)
    col = lax.broadcasted_iota(jnp.int32, (BLK, BLK), 1)
    return row, col


def pack(first, second):
    row, col = grids()
    body = jnp.where(row <= col, first, second)
    diag = jnp.sum(jnp.where(row == col, second, 0.0), axis=0, keepdims=True)
    return body, jnp.broadcast_to(diag, (PACK - BLK, BLK))


def unpack(body, diag):
    row, col = grids()
    turned = body.T
    first = jnp.where(row <= col, body, turned)
    second = jnp.where(row > col, body, jnp.where(row < col, turned, diag))
    return first, second


def fill_table(coords, table, which, me_r, me_c, places):
    classes = [coords[c, 1, 0] & 15 for c in places]
    zhi, x = me_r // 4, lax.rem(me_r, 4)
    keys = []
    for t in range(TILES):
        i, j = coords[me_c, 0, t], coords[me_c, 1, t]
        residue, half = i & 15, i >> 8
        place = jnp.int32(0)
        for n in range(16):
            place = jnp.where(classes[n] == residue, n, place)
        key = place * 2 + half
        keys.append(key)
        table[DIDX + t] = key
        dz, dx = ((j >> 6) - zhi) & 3, ((j >> 4) - x) & 3
        table[EIDX + t] = ((dx ^ (dx >> 1)) * 4 + (dz ^ (dz >> 1))) * 2 + (j >> 8)
        which[t] = jnp.where(i == j, 1 + half, 0)
    for n in range(32):
        slot = jnp.int32(TILES)
        for t in range(TILES):
            slot = jnp.where(keys[t] == n, t, slot)
        table[SRC + n] = slot


def diagonal_slots(coords, me_c):
    first, second = jnp.int32(0), jnp.int32(0)
    for t in range(TILES):
        i, j = coords[me_c, 0, t], coords[me_c, 1, t]
        first = jnp.where(jnp.logical_and(i == j, i < NB // 2), t, first)
        second = jnp.where(jnp.logical_and(i == j, i >= NB // 2), t, second)
    return first, second


def any_triple(coords, lanes, me_c):
    wide = (lanes[1:2] - lanes[0:1]) & (NB - 1)
    wide = jnp.where(wide == 0, -2, wide)
    offsets = [(coords[me_c, 1, t] - coords[me_c, 0, t]) & (NB - 1) for t in range(TILES)]
    found = jnp.zeros(wide.shape, jnp.int32)
    for s in range(TILES):
        for t in range(s, TILES):
            live = jnp.logical_and(offsets[s] != 0, offsets[t] != 0)
            both = jnp.where(live, (offsets[s] + offsets[t]) & (NB - 1), -1)
            found = found | (wide == both).astype(jnp.int32)
    return jnp.max(found)


def kernel(
    coords_hbm, dens_hbm, out_hbm, special, trace, flag, which,
    coords, table, lanes, dens, tiles, terms, dpack, epack, spack, mine, twins, summed, landed, sums,
    dfull, efull, sfull, square, outs, tcol, tz, tx,
    load_sem, d_send, d_recv, e_send, ez_recv, ex_recv, s_send, s_recv,
    x_send, x_recv, r_send, r_recv, t_send, t_recv, out_sem,
):
    me_r = lax.axis_index("row")
    me_c = lax.axis_index("col")
    core = lax.rem(me_c, 2)
    chip = me_c // 2
    zlo, y = chip // 4, lax.rem(chip, 4)
    zhi, x = me_r // 4, lax.rem(me_r, 4)
    chips = [lax.rem(zlo + dz, 2) * 4 + lax.rem(y + dy, 4) for dz, dy in CHIP_STEPS]
    same = [ch * 2 + core for ch in chips]
    places = same + [ch * 2 + 1 - core for ch in chips]
    twin = places[8]
    zs = [lax.rem(zhi + d, 4) * 4 + x for d in RING]
    xs = [zhi * 4 + lax.rem(x + d, 4) for d in RING]

    barrier = pltpu.get_barrier_semaphore()
    get_coords = pltpu.make_async_copy(coords_hbm.at[me_r], coords, load_sem.at[0])
    load = pltpu.make_async_copy(dens_hbm, dens, load_sem.at[1])
    get_lanes = pltpu.make_async_copy(coords_hbm.at[me_r, me_c], lanes, load_sem.at[2])
    get_coords.start()
    load.start()
    for b in (3, 2, 1):
        pl.semaphore_signal(barrier, inc=1, device_id={"row": zs[b]}, device_id_type=MESH)
    for n in range(15, 0, -1):
        pl.semaphore_signal(barrier, inc=1, device_id={"col": places[n]}, device_id_type=MESH)
    for a in (3, 2, 1):
        pl.semaphore_signal(barrier, inc=1, device_id={"row": xs[a]}, device_id_type=MESH)
    get_lanes.start()

    def to_col(src, dst, send, recv, c):
        return pltpu.make_async_remote_copy(
            src_ref=src, dst_ref=dst, send_sem=send, recv_sem=recv,
            device_id={"col": c}, device_id_type=MESH,
        )

    def to_row(src, dst, send, recv, r):
        return pltpu.make_async_remote_copy(
            src_ref=src, dst_ref=dst, send_sem=send, recv_sem=recv,
            device_id={"row": r}, device_id_type=MESH,
        )

    def spread_start(buf, send, recv):
        for k in range(1, 8):
            to_col(buf.at[0, 0], buf.at[0, CHIP_BACK[k]], send.at[0], recv.at[0], same[k]).start()

    def spread_seven(buf, send, recv):
        part = buf.at[0, 1:8]
        return to_col(part, part, send.at[0], recv.at[0], twin)

    def spread_twin(buf, send, recv):
        return to_col(buf.at[0], buf.at[1], send.at[1], recv.at[1], twin)

    def reduce_pack(rc, first):
        @each(first, 8)
        def _(k):
            n = rc * 8 + k
            body, diag = pack(terms[table[SRC + n * 2]].astype(F32), terms[table[SRC + n * 2 + 1]].astype(F32))
            mine[rc, k, 0:BLK] = body.astype(BF)
            mine[rc, k, BLK:PACK] = diag.astype(BF)

    def twin_copy(s):
        return to_col(mine.at[1], twins.at[s], x_send.at[s], x_recv.at[s], twin)

    def reduce_send(s):
        twin_copy(s).wait_recv()
        for k in range(7, -1, -1):
            summed[s, k] = (mine[0, k].astype(F32) + twins[s, k].astype(F32)).astype(BF)
            if k:
                to_col(summed.at[s, k], landed.at[s, CHIP_BACK[k]], r_send.at[s], r_recv.at[s], same[k]).start()

    def reduce_seven(s):
        return to_col(summed.at[s, 1:8], landed.at[s, 1:8], r_send.at[s], r_recv.at[s], twin)

    def reduce_end(s):
        reduce_seven(s).wait_recv()
        total = summed[s, 0].astype(F32)
        for k in range(1, 8):
            total = total + landed[s, k].astype(F32)
        sums[s] = total

    def expand(buf, n, m, full, at):
        first, second = unpack(buf[n, m, 0:BLK].astype(F32), buf[n, m, BLK:BLK + 1].astype(F32))
        full[at] = first.astype(BF)
        full[at + 1] = second.astype(BF)

    def expand_half(buf, rc, full):
        @each(0, 8)
        def _(k):
            expand(buf, rc, k, full, (rc * 8 + k) * 2)

    def fold(v):
        return jnp.sum(v.reshape(BLK // 8, 8, BLK), axis=0)

    get_coords.wait()
    own0, own1 = diagonal_slots(coords, me_c)
    load.wait()

    @each(0, TILES)
    def _(t):
        tiles[t] = dens[t].astype(BF)

    zero = jnp.zeros((BLK, BLK), BF)
    tiles[TILES] = zero
    terms[TILES] = zero
    body, diag = pack(tiles[own0].astype(F32), tiles[own1].astype(F32))
    body, diag = body.astype(BF), diag.astype(BF)
    dpack[0, 0, 0:BLK] = body
    dpack[0, 0, BLK:PACK] = diag
    epack[0, 0, 0:BLK] = body
    epack[0, 0, BLK:PACK] = diag

    pl.semaphore_wait(barrier, 21)
    for b in (1, 2, 3):
        to_row(epack.at[0, 0], epack.at[0, RING_BACK[b]], e_send.at[0], ez_recv.at[b // 3], zs[b]).start()

    def along_x(lo, hi, n):
        for a in (1, 2, 3):
            to_row(
                epack.at[0, lo:hi], epack.at[RING_BACK[a], lo:hi], e_send.at[1 + n], ex_recv.at[n], xs[a]
            ).start()

    def ring_wait(part, sem):
        return to_row(part, part, e_send.at[0], sem, me_r)

    along_x(0, 1, 0)

    fill_table(coords, table, which, me_r, me_c, places)

    @each(0, TILES)
    def _(t):
        b = tiles[t]
        terms[t] = dot_t(b, b).astype(BF)

    reduce_pack(1, 0)
    twin_copy(0).start()
    reduce_pack(0, 0)

    ring_wait(epack.at[0, 1:3], ez_recv.at[0]).wait_recv()
    along_x(1, 3, 0)
    reduce_send(0)
    spread_start(dpack, d_send, d_recv)
    ring_wait(epack.at[0, 3], ez_recv.at[1]).wait_recv()
    along_x(3, 4, 1)

    get_lanes.wait()
    flag[0, 0] = any_triple(coords, lanes, me_c)

    reduce_end(0)
    spack[0, 0] = sums[0].astype(BF)

    acc = jnp.zeros((8, BLK), F32)
    row, col = grids()
    parts = []
    for h, s in enumerate(unpack(sums[0, 0:BLK], sums[0, BLK:BLK + 1])):
        d = tiles[own0 if h == 0 else own1]
        rest = s - dot(d, d)
        acc = acc + fold(jnp.where(row == col, 3.0 * s, 0.0) - d.astype(F32) * (4.0 * rest + 2.0 * s))
        parts.append((d, s, rest))
    tcol[0] = acc
    for k in (8, 1, 2, 3, 9, 10, 11, 4, 5, 6, 12, 13, 14, 7, 15):
        back = k // 8 * 8 + CHIP_BACK[k % 8]
        to_col(tcol.at[0], tcol.at[back], t_send.at[0], t_recv.at[0], places[k]).start()
    spread_start(spack, s_send, s_recv)

    for h, (d, s, rest) in enumerate(parts):
        special[h] = 3.0 * s - 2.0 * (dot(d, rest.astype(BF)) + dot(s.astype(BF), d))

    for b in range(4):
        expand(epack, 0, b, efull, b * 2)
    ring_wait(epack.at[1:4, 0:3], ex_recv.at[0]).wait_recv()
    for a in range(1, 4):
        for b in range(3):
            expand(epack, a, b, efull, (a * 4 + b) * 2)
    twin_copy(0).wait_send()
    ring_wait(epack.at[1:4, 3], ex_recv.at[1]).wait_recv()
    for a in range(1, 4):
        expand(epack, a, 3, efull, (a * 4 + 3) * 2)

    @each(0, TILES)
    def _(t):
        b = tiles[t]
        f = dot(b, efull[table[EIDX + t]])
        square[t] = f
        terms[t] = dot_t(f.astype(BF), b).astype(BF)

    reduce_pack(1, 0)
    twin_copy(1).start()
    reduce_pack(0, 1)
    mine[0, 0] = jnp.zeros((PACK, BLK), BF)

    spread_seven(dpack, d_send, d_recv).wait_recv()
    spread_twin(dpack, d_send, d_recv).start()
    expand_half(dpack, 0, dfull)

    reduce_send(1)

    tcol_all = to_col(tcol.at[1:16], tcol.at[1:16], t_send.at[0], t_recv.at[0], twin)
    tcol_all.wait_recv()
    tz[0] = jnp.sum(tcol[...], axis=0)
    for b in (1, 2, 3):
        to_row(tz.at[0], tz.at[RING_BACK[b]], t_send.at[1], t_recv.at[1], zs[b]).start()

    spread_twin(dpack, d_send, d_recv).wait_recv()
    expand_half(dpack, 1, dfull)

    @each(0, TILES)
    def _(t):
        s = square[t] + dot(dfull[table[DIDX + t]], tiles[t])
        outs[t] = 3.0 * s - 2.0 * dot(s.astype(BF), efull[table[EIDX + t]])

    spread_seven(spack, s_send, s_recv).wait_recv()
    spread_twin(spack, s_send, s_recv).start()
    expand_half(spack, 0, sfull)

    tz_three = to_row(tz.at[1:4], tz.at[1:4], t_send.at[1], t_recv.at[1], me_r)
    tz_three.wait_recv()
    tx[0] = jnp.sum(tz[...], axis=0)
    for a in (1, 2, 3):
        to_row(tx.at[0], tx.at[RING_BACK[a]], t_send.at[2], t_recv.at[2], xs[a]).start()

    spread_twin(spack, s_send, s_recv).wait_recv()
    expand_half(spack, 1, sfull)

    @each(0, TILES)
    def _(t):
        outs[t] = outs[t] - 2.0 * dot(sfull[table[DIDX + t]], tiles[t])

    store = pltpu.make_async_copy(outs, out_hbm, out_sem)
    store.start()

    reduce_end(1)
    for h, q in enumerate(unpack(sums[1, 0:BLK], sums[1, BLK:BLK + 1])):
        special[h] = special[h] - 2.0 * q

    for buf, send, recv in ((dpack, d_send, d_recv), (spack, s_send, s_recv)):
        spread_seven(buf, send, recv).wait_send()
        spread_twin(buf, send, recv).wait_send()
    ring_wait(epack.at[0, 1:4], ez_recv.at[0]).wait_send()
    part = epack.at[1:4, 0:3]
    to_row(part, part, e_send.at[1], ex_recv.at[0], me_r).wait_send()
    part = epack.at[1:4, 3]
    to_row(part, part, e_send.at[2], ex_recv.at[1], me_r).wait_send()
    twin_copy(1).wait_send()
    reduce_seven(0).wait_send()
    reduce_seven(1).wait_send()
    tcol_all.wait_send()
    tz_three.wait_send()

    tx_three = to_row(tx.at[1:4], tx.at[1:4], t_send.at[2], t_recv.at[2], me_r)
    tx_three.wait_recv()
    trace[0, 0] = jnp.sum(tx[...]) / (NB * BLK)
    tx_three.wait_send()
    store.wait()


def fast_call(coords, dens):
    dma = pltpu.SemaphoreType.DMA
    pair = (2, 8, PACK, BLK)
    smem = pl.BlockSpec(memory_space=pltpu.SMEM)
    return pl.pallas_call(
        kernel,
        out_shape=(
            jax.ShapeDtypeStruct((TILES, BLK, BLK), F32),
            jax.ShapeDtypeStruct((2, BLK, BLK), F32),
            jax.ShapeDtypeStruct((1, 1), F32),
            jax.ShapeDtypeStruct((1, 1), jnp.int32),
            jax.ShapeDtypeStruct((TILES,), jnp.int32),
        ),
        in_specs=[pl.BlockSpec(memory_space=pl.ANY), pl.BlockSpec(memory_space=pl.ANY)],
        out_specs=(
            pl.BlockSpec(memory_space=pl.ANY), pl.BlockSpec(memory_space=pltpu.VMEM), smem, smem, smem,
        ),
        scratch_shapes=[
            pltpu.SMEM((16, 2, TILES), jnp.int32),
            pltpu.SMEM((TABLE,), jnp.int32),
            pltpu.VMEM((2, TILES), jnp.int32),
            pltpu.VMEM((TILES, BLK, BLK), F32),
            pltpu.VMEM((TILES + 1, BLK, BLK), BF),
            pltpu.VMEM((TILES + 1, BLK, BLK), BF),
            pltpu.VMEM(pair, BF),
            pltpu.VMEM((4, 4, PACK, BLK), BF),
            pltpu.VMEM(pair, BF),
            pltpu.VMEM(pair, BF),
            pltpu.VMEM(pair, BF),
            pltpu.VMEM(pair, BF),
            pltpu.VMEM(pair, BF),
            pltpu.VMEM((2, PACK, BLK), F32),
            pltpu.VMEM((32, BLK, BLK), BF),
            pltpu.VMEM((32, BLK, BLK), BF),
            pltpu.VMEM((32, BLK, BLK), BF),
            pltpu.VMEM((TILES, BLK, BLK), F32),
            pltpu.VMEM((TILES, BLK, BLK), F32),
            pltpu.VMEM((16, 8, BLK), F32),
            pltpu.VMEM((4, 8, BLK), F32),
            pltpu.VMEM((4, 8, BLK), F32),
            dma((3,)),
            dma((2,)), dma((2,)),
            dma((3,)), dma((2,)), dma((2,)),
            dma((2,)), dma((2,)),
            dma((2,)), dma((2,)),
            dma((2,)), dma((2,)),
            dma((3,)), dma((3,)),
            dma(()),
        ],
        compiler_params=pltpu.CompilerParams(
            collective_id=0, has_side_effects=True, vmem_limit_bytes=40 * 1024 * 1024
        ),
    )(coords, dens)


def pair_lookup(own_coords, targets, mirror_coords):
    own_rows = own_coords[:, 0]
    own_cols = own_coords[:, 1]
    target_row = targets[:, 0]
    target_col = targets[:, 1]
    first = own_rows[None, :] == target_row[:, None]
    has_first = jnp.any(first, axis=1)
    left_slot = jnp.argmax(first.astype(jnp.int32), axis=1)
    inner = own_cols[left_slot]
    second = (mirror_coords[None, :, 0] == target_col[:, None]) & (
        mirror_coords[None, :, 1] == inner[:, None]
    )
    second = second & has_first[:, None]
    keep = jnp.any(second, axis=1)
    right_slot = jnp.argmax(second.astype(jnp.int32), axis=1)
    return (left_slot, right_slot, keep)


def to_all(value, axis):
    return lax.all_to_all(jnp.broadcast_to(value[None], (16,) + value.shape), axis, 0, 0)


def scattered_product(left, mirror, left_slot, right_slot, keep):
    weight = keep.astype(F32)
    left_rows = jnp.take(left, left_slot, axis=0)
    right_rows = jnp.take(mirror, right_slot, axis=0)
    result = jnp.einsum("nik,njk->nij", left_rows, right_rows, preferred_element_type=F32)
    result = (result * weight[:, None, None]).astype(BF).reshape(16, TILES, BLK, BLK)
    return jnp.sum(lax.all_to_all(result, "col", 0, 0).astype(F32), axis=0)


def general(density, tile_coords):
    own_tiles = density[0, 0]
    own_low = own_tiles.astype(BF)
    my_row = lax.axis_index("row")
    my_col = lax.axis_index("col")
    row_table = jnp.take(tile_coords, my_row, axis=0)
    own_coords = jnp.take(row_table, my_col, axis=0)
    row_flat = row_table.reshape(-1, 2)
    col_flat = jnp.take(tile_coords, my_col, axis=1).reshape(-1, 2)
    mirror = to_all(own_low, "row").reshape(-1, BLK, BLK)
    own_diag = own_coords[:, 0] == own_coords[:, 1]
    left_slot, right_slot, keep = pair_lookup(own_coords, row_flat, col_flat)
    square = scattered_product(own_low, mirror, left_slot, right_slot, keep)
    square_low = square.astype(BF)
    cube = scattered_product(square_low, mirror, left_slot, right_slot, keep)
    purified = 3.0 * square - 2.0 * cube
    total = jnp.sum(jnp.where(own_diag, jnp.einsum("nii->n", purified), 0.0))
    total = jnp.sum(to_all(jnp.sum(to_all(total, "col")), "row"))
    return purified, total / (NB * BLK)


def per_device(density, tile_coords):
    out, special, trace, flag, which = fast_call(tile_coords.transpose(0, 1, 3, 2), density[0, 0])
    which = which[:, None, None]
    out = jnp.where(which == 0, out, jnp.where(which == 1, special[0][None], special[1][None]))
    out, mean_diagonal = lax.cond(
        flag[0, 0] > 0,
        lambda out, trace: general(density, tile_coords),
        lambda out, trace: (out, trace),
        out, trace[0, 0],
    )
    return out[None, None], mean_diagonal


def solution(mesh):
    return jax.shard_map(
        per_device,
        mesh=mesh,
        in_specs=(P("row", "col", None, None, None), P()),
        out_specs=(P("row", "col", None, None, None), P()),
        check_vma=False,
    )
```

```python
import jax
import jax.numpy as jnp
from jax import lax
from jax.experimental import pallas as pl
from jax.experimental.pallas import tpu as pltpu
from jax.sharding import PartitionSpec as P

NB = 512
BLK = 128
TILES = 18
PACK = BLK + 16
BF = jnp.bfloat16
F32 = jnp.float32
MESH = pl.DeviceIdType.MESH

CHIP_STEPS = ((0, 0), (0, 1), (0, 3), (1, 0), (0, 2), (1, 1), (1, 3), (1, 2))
CHIP_BACK = tuple(CHIP_STEPS.index((-dz % 2, -dy % 4)) for dz, dy in CHIP_STEPS)
RING = (0, 1, 3, 2)
RING_BACK = tuple(RING.index(-d % 4) for d in RING)

SRC, DIDX, EIDX, TABLE = 0, 32, 64, 96


def dot(a, b):
    return jnp.dot(a, b, preferred_element_type=F32)


def dot_t(a, b):
    return lax.dot_general(a, b, (((1,), (1,)), ((), ())), preferred_element_type=F32)


def each(lo, hi):
    return pl.loop(lo, hi, unroll=True)


def grids():
    row = lax.broadcasted_iota(jnp.int32, (BLK, BLK), 0)
    col = lax.broadcasted_iota(jnp.int32, (BLK, BLK), 1)
    return row, col


def pack(first, second):
    row, col = grids()
    body = jnp.where(row <= col, first, second)
    diag = jnp.sum(jnp.where(row == col, second, 0.0), axis=0, keepdims=True)
    return body, jnp.broadcast_to(diag, (PACK - BLK, BLK))


def unpack(body, diag):
    row, col = grids()
    turned = body.T
    first = jnp.where(row <= col, body, turned)
    second = jnp.where(row > col, body, jnp.where(row < col, turned, diag))
    return first, second


def fill_table(coords, table, which, me_r, me_c, places):
    classes = [coords[c, 1, 0] & 15 for c in places]
    zhi, x = me_r // 4, lax.rem(me_r, 4)
    keys = []
    for t in range(TILES):
        i, j = coords[me_c, 0, t], coords[me_c, 1, t]
        residue, half = i & 15, i >> 8
        place = jnp.int32(0)
        for n in range(16):
            place = jnp.where(classes[n] == residue, n, place)
        key = place * 2 + half
        keys.append(key)
        table[DIDX + t] = key
        dz, dx = ((j >> 6) - zhi) & 3, ((j >> 4) - x) & 3
        table[EIDX + t] = ((dx ^ (dx >> 1)) * 4 + (dz ^ (dz >> 1))) * 2 + (j >> 8)
        which[t] = jnp.where(i == j, 1 + half, 0)
    for n in range(32):
        slot = jnp.int32(TILES)
        for t in range(TILES):
            slot = jnp.where(keys[t] == n, t, slot)
        table[SRC + n] = slot


def diagonal_slots(coords, me_c):
    first, second = jnp.int32(0), jnp.int32(0)
    for t in range(TILES):
        i, j = coords[me_c, 0, t], coords[me_c, 1, t]
        first = jnp.where(jnp.logical_and(i == j, i < NB // 2), t, first)
        second = jnp.where(jnp.logical_and(i == j, i >= NB // 2), t, second)
    return first, second


def any_triple(coords, lanes, me_c):
    wide = (lanes[1:2] - lanes[0:1]) & (NB - 1)
    wide = jnp.where(wide == 0, -2, wide)
    offsets = [(coords[me_c, 1, t] - coords[me_c, 0, t]) & (NB - 1) for t in range(TILES)]
    found = jnp.zeros(wide.shape, jnp.int32)
    for s in range(TILES):
        for t in range(s, TILES):
            live = jnp.logical_and(offsets[s] != 0, offsets[t] != 0)
            both = jnp.where(live, (offsets[s] + offsets[t]) & (NB - 1), -1)
            found = found | (wide == both).astype(jnp.int32)
    return jnp.max(found)


def kernel(
    coords_hbm, dens_hbm, out_hbm, special, trace, flag, which,
    coords, table, lanes, dens, tiles, terms, dpack, epack, spack, mine, twins, summed, landed, sums,
    dfull, efull, sfull, square, outs, tcol, tz, tx,
    load_sem, d_send, d_recv, e_send, ez_recv, ex_recv, s_send, s_recv,
    x_send, x_recv, r_send, r_recv, t_send, t_recv, out_sem,
):
    me_r = lax.axis_index("row")
    me_c = lax.axis_index("col")
    core = lax.rem(me_c, 2)
    chip = me_c // 2
    zlo, y = chip // 4, lax.rem(chip, 4)
    zhi, x = me_r // 4, lax.rem(me_r, 4)
    chips = [lax.rem(zlo + dz, 2) * 4 + lax.rem(y + dy, 4) for dz, dy in CHIP_STEPS]
    same = [ch * 2 + core for ch in chips]
    places = same + [ch * 2 + 1 - core for ch in chips]
    twin = places[8]
    zs = [lax.rem(zhi + d, 4) * 4 + x for d in RING]
    xs = [zhi * 4 + lax.rem(x + d, 4) for d in RING]

    barrier = pltpu.get_barrier_semaphore()
    get_coords = pltpu.make_async_copy(coords_hbm.at[me_r], coords, load_sem.at[0])
    load = pltpu.make_async_copy(dens_hbm, dens, load_sem.at[1])
    get_lanes = pltpu.make_async_copy(coords_hbm.at[me_r, me_c], lanes, load_sem.at[2])
    get_coords.start()
    load.start()
    for b in (3, 2, 1):
        pl.semaphore_signal(barrier, inc=1, device_id={"row": zs[b]}, device_id_type=MESH)
    for n in range(15, 0, -1):
        pl.semaphore_signal(barrier, inc=1, device_id={"col": places[n]}, device_id_type=MESH)
    for a in (3, 2, 1):
        pl.semaphore_signal(barrier, inc=1, device_id={"row": xs[a]}, device_id_type=MESH)
    get_lanes.start()

    def to_col(src, dst, send, recv, c):
        return pltpu.make_async_remote_copy(
            src_ref=src, dst_ref=dst, send_sem=send, recv_sem=recv,
            device_id={"col": c}, device_id_type=MESH,
        )

    def to_row(src, dst, send, recv, r):
        return pltpu.make_async_remote_copy(
            src_ref=src, dst_ref=dst, send_sem=send, recv_sem=recv,
            device_id={"row": r}, device_id_type=MESH,
        )

    def spread_start(buf, send, recv):
        for k in range(1, 8):
            to_col(buf.at[0, 0], buf.at[0, CHIP_BACK[k]], send.at[0], recv.at[0], same[k]).start()

    def spread_seven(buf, send, recv):
        part = buf.at[0, 1:8]
        return to_col(part, part, send.at[0], recv.at[0], twin)

    def spread_twin(buf, send, recv):
        return to_col(buf.at[0], buf.at[1], send.at[1], recv.at[1], twin)

    def reduce_pack(rc, first):
        @each(first, 8)
        def _(k):
            n = rc * 8 + k
            body, diag = pack(terms[table[SRC + n * 2]].astype(F32), terms[table[SRC + n * 2 + 1]].astype(F32))
            mine[rc, k, 0:BLK] = body.astype(BF)
            mine[rc, k, BLK:PACK] = diag.astype(BF)

    def twin_copy(s):
        return to_col(mine.at[1], twins.at[s], x_send.at[s], x_recv.at[s], twin)

    def reduce_send(s):
        twin_copy(s).wait_recv()
        for k in range(7, -1, -1):
            summed[s, k] = (mine[0, k].astype(F32) + twins[s, k].astype(F32)).astype(BF)
            if k:
                to_col(summed.at[s, k], landed.at[s, CHIP_BACK[k]], r_send.at[s], r_recv.at[s], same[k]).start()

    def reduce_seven(s):
        return to_col(summed.at[s, 1:8], landed.at[s, 1:8], r_send.at[s], r_recv.at[s], twin)

    def reduce_end(s):
        reduce_seven(s).wait_recv()
        total = summed[s, 0].astype(F32)
        for k in range(1, 8):
            total = total + landed[s, k].astype(F32)
        sums[s] = total

    def expand(buf, n, m, full, at):
        first, second = unpack(buf[n, m, 0:BLK].astype(F32), buf[n, m, BLK:BLK + 1].astype(F32))
        full[at] = first.astype(BF)
        full[at + 1] = second.astype(BF)

    def expand_half(buf, rc, full):
        @each(0, 8)
        def _(k):
            expand(buf, rc, k, full, (rc * 8 + k) * 2)

    def fold(v):
        return jnp.sum(v.reshape(BLK // 8, 8, BLK), axis=0)

    get_coords.wait()
    own0, own1 = diagonal_slots(coords, me_c)
    load.wait()

    @each(0, TILES)
    def _(t):
        tiles[t] = dens[t].astype(BF)

    zero = jnp.zeros((BLK, BLK), BF)
    tiles[TILES] = zero
    terms[TILES] = zero
    body, diag = pack(tiles[own0].astype(F32), tiles[own1].astype(F32))
    body, diag = body.astype(BF), diag.astype(BF)
    dpack[0, 0, 0:BLK] = body
    dpack[0, 0, BLK:PACK] = diag
    epack[0, 0, 0:BLK] = body
    epack[0, 0, BLK:PACK] = diag

    pl.semaphore_wait(barrier, 21)
    for b in (1, 2, 3):
        to_row(epack.at[0, 0], epack.at[0, RING_BACK[b]], e_send.at[0], ez_recv.at[b // 3], zs[b]).start()

    def along_x(lo, hi, n):
        for a in (1, 2, 3):
            to_row(
                epack.at[0, lo:hi], epack.at[RING_BACK[a], lo:hi], e_send.at[1 + n], ex_recv.at[n], xs[a]
            ).start()

    def ring_wait(part, sem):
        return to_row(part, part, e_send.at[0], sem, me_r)

    along_x(0, 1, 0)

    fill_table(coords, table, which, me_r, me_c, places)

    @each(0, TILES)
    def _(t):
        b = tiles[t]
        terms[t] = dot_t(b, b).astype(BF)

    reduce_pack(1, 0)
    twin_copy(0).start()
    reduce_pack(0, 0)

    ring_wait(epack.at[0, 1:3], ez_recv.at[0]).wait_recv()
    along_x(1, 3, 0)
    reduce_send(0)
    spread_start(dpack, d_send, d_recv)
    ring_wait(epack.at[0, 3], ez_recv.at[1]).wait_recv()
    along_x(3, 4, 1)

    get_lanes.wait()
    flag[0, 0] = any_triple(coords, lanes, me_c)

    reduce_end(0)
    spack[0, 0] = sums[0].astype(BF)

    acc = jnp.zeros((8, BLK), F32)
    row, col = grids()
    parts = []
    for h, s in enumerate(unpack(sums[0, 0:BLK], sums[0, BLK:BLK + 1])):
        d = tiles[own0 if h == 0 else own1]
        rest = s - dot(d, d)
        acc = acc + fold(jnp.where(row == col, 3.0 * s, 0.0) - d.astype(F32) * (4.0 * rest + 2.0 * s))
        parts.append((d, s, rest))
    tcol[0] = acc
    for k in (8, 1, 2, 3, 9, 10, 11, 4, 5, 6, 12, 13, 14, 7, 15):
        back = k // 8 * 8 + CHIP_BACK[k % 8]
        to_col(tcol.at[0], tcol.at[back], t_send.at[0], t_recv.at[0], places[k]).start()
    spread_start(spack, s_send, s_recv)

    for h, (d, s, rest) in enumerate(parts):
        special[h] = 3.0 * s - 2.0 * (dot(d, rest.astype(BF)) + dot(s.astype(BF), d))

    for b in range(4):
        expand(epack, 0, b, efull, b * 2)
    ring_wait(epack.at[1:4, 0:3], ex_recv.at[0]).wait_recv()
    for a in range(1, 4):
        for b in range(3):
            expand(epack, a, b, efull, (a * 4 + b) * 2)
    twin_copy(0).wait_send()
    ring_wait(epack.at[1:4, 3], ex_recv.at[1]).wait_recv()
    for a in range(1, 4):
        expand(epack, a, 3, efull, (a * 4 + 3) * 2)

    @each(0, TILES)
    def _(t):
        b = tiles[t]
        f = dot(b, efull[table[EIDX + t]])
        square[t] = f
        terms[t] = dot_t(f.astype(BF), b).astype(BF)

    reduce_pack(1, 0)
    twin_copy(1).start()
    reduce_pack(0, 1)
    mine[0, 0] = jnp.zeros((PACK, BLK), BF)

    spread_seven(dpack, d_send, d_recv).wait_recv()
    spread_twin(dpack, d_send, d_recv).start()
    expand_half(dpack, 0, dfull)

    tcol_all = to_col(tcol.at[1:16], tcol.at[1:16], t_send.at[0], t_recv.at[0], twin)
    tcol_all.wait_recv()
    tz[0] = jnp.sum(tcol[...], axis=0)
    for b in (1, 2, 3):
        to_row(tz.at[0], tz.at[RING_BACK[b]], t_send.at[1], t_recv.at[1], zs[b]).start()

    reduce_send(1)

    spread_twin(dpack, d_send, d_recv).wait_recv()
    expand_half(dpack, 1, dfull)

    @each(0, TILES)
    def _(t):
        s = square[t] + dot(dfull[table[DIDX + t]], tiles[t])
        outs[t] = 3.0 * s - 2.0 * dot(s.astype(BF), efull[table[EIDX + t]])

    spread_seven(spack, s_send, s_recv).wait_recv()
    spread_twin(spack, s_send, s_recv).start()
    expand_half(spack, 0, sfull)

    tz_three = to_row(tz.at[1:4], tz.at[1:4], t_send.at[1], t_recv.at[1], me_r)
    tz_three.wait_recv()
    tx[0] = jnp.sum(tz[...], axis=0)
    for a in (1, 2, 3):
        to_row(tx.at[0], tx.at[RING_BACK[a]], t_send.at[2], t_recv.at[2], xs[a]).start()

    spread_twin(spack, s_send, s_recv).wait_recv()
    expand_half(spack, 1, sfull)

    @each(0, TILES)
    def _(t):
        outs[t] = outs[t] - 2.0 * dot(sfull[table[DIDX + t]], tiles[t])

    store = pltpu.make_async_copy(outs, out_hbm, out_sem)
    store.start()

    reduce_end(1)
    for h, q in enumerate(unpack(sums[1, 0:BLK], sums[1, BLK:BLK + 1])):
        special[h] = special[h] - 2.0 * q

    for buf, send, recv in ((dpack, d_send, d_recv), (spack, s_send, s_recv)):
        spread_seven(buf, send, recv).wait_send()
        spread_twin(buf, send, recv).wait_send()
    ring_wait(epack.at[0, 1:4], ez_recv.at[0]).wait_send()
    part = epack.at[1:4, 0:3]
    to_row(part, part, e_send.at[1], ex_recv.at[0], me_r).wait_send()
    part = epack.at[1:4, 3]
    to_row(part, part, e_send.at[2], ex_recv.at[1], me_r).wait_send()
    twin_copy(1).wait_send()
    reduce_seven(0).wait_send()
    reduce_seven(1).wait_send()
    tcol_all.wait_send()
    tz_three.wait_send()

    tx_three = to_row(tx.at[1:4], tx.at[1:4], t_send.at[2], t_recv.at[2], me_r)
    tx_three.wait_recv()
    trace[0, 0] = jnp.sum(tx[...]) / (NB * BLK)
    tx_three.wait_send()
    store.wait()


def fast_call(coords, dens):
    dma = pltpu.SemaphoreType.DMA
    pair = (2, 8, PACK, BLK)
    smem = pl.BlockSpec(memory_space=pltpu.SMEM)
    return pl.pallas_call(
        kernel,
        out_shape=(
            jax.ShapeDtypeStruct((TILES, BLK, BLK), F32),
            jax.ShapeDtypeStruct((2, BLK, BLK), F32),
            jax.ShapeDtypeStruct((1, 1), F32),
            jax.ShapeDtypeStruct((1, 1), jnp.int32),
            jax.ShapeDtypeStruct((TILES,), jnp.int32),
        ),
        in_specs=[pl.BlockSpec(memory_space=pl.ANY), pl.BlockSpec(memory_space=pl.ANY)],
        out_specs=(
            pl.BlockSpec(memory_space=pl.ANY), pl.BlockSpec(memory_space=pltpu.VMEM), smem, smem, smem,
        ),
        scratch_shapes=[
            pltpu.SMEM((16, 2, TILES), jnp.int32),
            pltpu.SMEM((TABLE,), jnp.int32),
            pltpu.VMEM((2, TILES), jnp.int32),
            pltpu.VMEM((TILES, BLK, BLK), F32),
            pltpu.VMEM((TILES + 1, BLK, BLK), BF),
            pltpu.VMEM((TILES + 1, BLK, BLK), BF),
            pltpu.VMEM(pair, BF),
            pltpu.VMEM((4, 4, PACK, BLK), BF),
            pltpu.VMEM(pair, BF),
            pltpu.VMEM(pair, BF),
            pltpu.VMEM(pair, BF),
            pltpu.VMEM(pair, BF),
            pltpu.VMEM(pair, BF),
            pltpu.VMEM((2, PACK, BLK), F32),
            pltpu.VMEM((32, BLK, BLK), BF),
            pltpu.VMEM((32, BLK, BLK), BF),
            pltpu.VMEM((32, BLK, BLK), BF),
            pltpu.VMEM((TILES, BLK, BLK), F32),
            pltpu.VMEM((TILES, BLK, BLK), F32),
            pltpu.VMEM((16, 8, BLK), F32),
            pltpu.VMEM((4, 8, BLK), F32),
            pltpu.VMEM((4, 8, BLK), F32),
            dma((3,)),
            dma((2,)), dma((2,)),
            dma((3,)), dma((2,)), dma((2,)),
            dma((2,)), dma((2,)),
            dma((2,)), dma((2,)),
            dma((2,)), dma((2,)),
            dma((3,)), dma((3,)),
            dma(()),
        ],
        compiler_params=pltpu.CompilerParams(
            collective_id=0, has_side_effects=True, vmem_limit_bytes=40 * 1024 * 1024
        ),
    )(coords, dens)


def pair_lookup(own_coords, targets, mirror_coords):
    own_rows = own_coords[:, 0]
    own_cols = own_coords[:, 1]
    target_row = targets[:, 0]
    target_col = targets[:, 1]
    first = own_rows[None, :] == target_row[:, None]
    has_first = jnp.any(first, axis=1)
    left_slot = jnp.argmax(first.astype(jnp.int32), axis=1)
    inner = own_cols[left_slot]
    second = (mirror_coords[None, :, 0] == target_col[:, None]) & (
        mirror_coords[None, :, 1] == inner[:, None]
    )
    second = second & has_first[:, None]
    keep = jnp.any(second, axis=1)
    right_slot = jnp.argmax(second.astype(jnp.int32), axis=1)
    return (left_slot, right_slot, keep)


def to_all(value, axis):
    return lax.all_to_all(jnp.broadcast_to(value[None], (16,) + value.shape), axis, 0, 0)


def scattered_product(left, mirror, left_slot, right_slot, keep):
    weight = keep.astype(F32)
    left_rows = jnp.take(left, left_slot, axis=0)
    right_rows = jnp.take(mirror, right_slot, axis=0)
    result = jnp.einsum("nik,njk->nij", left_rows, right_rows, preferred_element_type=F32)
    result = (result * weight[:, None, None]).astype(BF).reshape(16, TILES, BLK, BLK)
    return jnp.sum(lax.all_to_all(result, "col", 0, 0).astype(F32), axis=0)


def general(density, tile_coords):
    own_tiles = density[0, 0]
    own_low = own_tiles.astype(BF)
    my_row = lax.axis_index("row")
    my_col = lax.axis_index("col")
    row_table = jnp.take(tile_coords, my_row, axis=0)
    own_coords = jnp.take(row_table, my_col, axis=0)
    row_flat = row_table.reshape(-1, 2)
    col_flat = jnp.take(tile_coords, my_col, axis=1).reshape(-1, 2)
    mirror = to_all(own_low, "row").reshape(-1, BLK, BLK)
    own_diag = own_coords[:, 0] == own_coords[:, 1]
    left_slot, right_slot, keep = pair_lookup(own_coords, row_flat, col_flat)
    square = scattered_product(own_low, mirror, left_slot, right_slot, keep)
    square_low = square.astype(BF)
    cube = scattered_product(square_low, mirror, left_slot, right_slot, keep)
    purified = 3.0 * square - 2.0 * cube
    total = jnp.sum(jnp.where(own_diag, jnp.einsum("nii->n", purified), 0.0))
    total = jnp.sum(to_all(jnp.sum(to_all(total, "col")), "row"))
    return purified, total / (NB * BLK)


def per_device(density, tile_coords):
    out, special, trace, flag, which = fast_call(tile_coords.transpose(0, 1, 3, 2), density[0, 0])
    which = which[:, None, None]
    out = jnp.where(which == 0, out, jnp.where(which == 1, special[0][None], special[1][None]))
    out, mean_diagonal = lax.cond(
        flag[0, 0] > 0,
        lambda out, trace: general(density, tile_coords),
        lambda out, trace: (out, trace),
        out, trace[0, 0],
    )
    return out[None, None], mean_diagonal


def solution(mesh):
    return jax.shard_map(
        per_device,
        mesh=mesh,
        in_specs=(P("row", "col", None, None, None), P()),
        out_specs=(P("row", "col", None, None, None), P()),
        check_vma=False,
    )
```

```python
import jax
import jax.numpy as jnp
from jax import lax
from jax.experimental import pallas as pl
from jax.experimental.pallas import tpu as pltpu
from jax.sharding import PartitionSpec as P

NB = 512
BLK = 128
TILES = 18
PACK = BLK + 16
BF = jnp.bfloat16
F32 = jnp.float32
MESH = pl.DeviceIdType.MESH

CHIP_STEPS = ((0, 0), (0, 1), (0, 3), (1, 0), (0, 2), (1, 1), (1, 3), (1, 2))
CHIP_BACK = tuple(CHIP_STEPS.index((-dz % 2, -dy % 4)) for dz, dy in CHIP_STEPS)
RING = (0, 1, 3, 2)
RING_BACK = tuple(RING.index(-d % 4) for d in RING)

SRC, DIDX, EIDX, TABLE = 0, 32, 64, 96


def dot(a, b):
    return jnp.dot(a, b, preferred_element_type=F32)


def dot_t(a, b):
    return lax.dot_general(a, b, (((1,), (1,)), ((), ())), preferred_element_type=F32)


def each(lo, hi):
    return pl.loop(lo, hi, unroll=True)


def grids():
    row = lax.broadcasted_iota(jnp.int32, (BLK, BLK), 0)
    col = lax.broadcasted_iota(jnp.int32, (BLK, BLK), 1)
    return row, col


def pack(first, second):
    row, col = grids()
    body = jnp.where(row <= col, first, second)
    diag = jnp.sum(jnp.where(row == col, second, 0.0), axis=0, keepdims=True)
    return body, jnp.broadcast_to(diag, (PACK - BLK, BLK))


def unpack(body, diag):
    row, col = grids()
    turned = body.T
    first = jnp.where(row <= col, body, turned)
    second = jnp.where(row > col, body, jnp.where(row < col, turned, diag))
    return first, second


def fill_table(coords, table, which, me_r, me_c, places):
    classes = [coords[c, 1, 0] & 15 for c in places]
    zhi, x = me_r // 4, lax.rem(me_r, 4)
    keys = []
    for t in range(TILES):
        i, j = coords[me_c, 0, t], coords[me_c, 1, t]
        residue, half = i & 15, i >> 8
        place = jnp.int32(0)
        for n in range(16):
            place = jnp.where(classes[n] == residue, n, place)
        key = place * 2 + half
        keys.append(key)
        table[DIDX + t] = key
        dz, dx = ((j >> 6) - zhi) & 3, ((j >> 4) - x) & 3
        table[EIDX + t] = ((dx ^ (dx >> 1)) * 4 + (dz ^ (dz >> 1))) * 2 + (j >> 8)
        which[t] = jnp.where(i == j, 1 + half, 0)
    for n in range(32):
        slot = jnp.int32(TILES)
        for t in range(TILES):
            slot = jnp.where(keys[t] == n, t, slot)
        table[SRC + n] = slot


def diagonal_slots(coords, me_c):
    first, second = jnp.int32(0), jnp.int32(0)
    for t in range(TILES):
        i, j = coords[me_c, 0, t], coords[me_c, 1, t]
        first = jnp.where(jnp.logical_and(i == j, i < NB // 2), t, first)
        second = jnp.where(jnp.logical_and(i == j, i >= NB // 2), t, second)
    return first, second


def any_triple(coords, lanes, me_c):
    wide = (lanes[1:2] - lanes[0:1]) & (NB - 1)
    wide = jnp.where(wide == 0, -2, wide)
    offsets = [(coords[me_c, 1, t] - coords[me_c, 0, t]) & (NB - 1) for t in range(TILES)]
    found = jnp.zeros(wide.shape, jnp.int32)
    for s in range(TILES):
        for t in range(s, TILES):
            live = jnp.logical_and(offsets[s] != 0, offsets[t] != 0)
            both = jnp.where(live, (offsets[s] + offsets[t]) & (NB - 1), -1)
            found = found | (wide == both).astype(jnp.int32)
    return jnp.max(found)


def kernel(
    coords_hbm, dens_hbm, out_hbm, special, trace, flag, which,
    coords, table, lanes, dens, tiles, terms, dpack, epack, spack, mine, twins, summed, landed, sums,
    dfull, efull, sfull, square, outs, tcol, tz, tx,
    load_sem, d_send, d_recv, e_send, ez_recv, ex_recv, s_send, s_recv,
    x_send, x_recv, r_send, r_recv, t_send, t_recv, out_sem,
):
    me_r = lax.axis_index("row")
    me_c = lax.axis_index("col")
    core = lax.rem(me_c, 2)
    chip = me_c // 2
    zlo, y = chip // 4, lax.rem(chip, 4)
    zhi, x = me_r // 4, lax.rem(me_r, 4)
    chips = [lax.rem(zlo + dz, 2) * 4 + lax.rem(y + dy, 4) for dz, dy in CHIP_STEPS]
    same = [ch * 2 + core for ch in chips]
    places = same + [ch * 2 + 1 - core for ch in chips]
    twin = places[8]
    zs = [lax.rem(zhi + d, 4) * 4 + x for d in RING]
    xs = [zhi * 4 + lax.rem(x + d, 4) for d in RING]

    barrier = pltpu.get_barrier_semaphore()
    get_coords = pltpu.make_async_copy(coords_hbm.at[me_r], coords, load_sem.at[0])
    load = pltpu.make_async_copy(dens_hbm, dens, load_sem.at[1])
    get_lanes = pltpu.make_async_copy(coords_hbm.at[me_r, me_c], lanes, load_sem.at[2])
    get_coords.start()
    load.start()
    for b in (3, 2, 1):
        pl.semaphore_signal(barrier, inc=1, device_id={"row": zs[b]}, device_id_type=MESH)
    for n in range(15, 0, -1):
        pl.semaphore_signal(barrier, inc=1, device_id={"col": places[n]}, device_id_type=MESH)
    for a in (3, 2, 1):
        pl.semaphore_signal(barrier, inc=1, device_id={"row": xs[a]}, device_id_type=MESH)
    get_lanes.start()

    def to_col(src, dst, send, recv, c):
        return pltpu.make_async_remote_copy(
            src_ref=src, dst_ref=dst, send_sem=send, recv_sem=recv,
            device_id={"col": c}, device_id_type=MESH,
        )

    def to_row(src, dst, send, recv, r):
        return pltpu.make_async_remote_copy(
            src_ref=src, dst_ref=dst, send_sem=send, recv_sem=recv,
            device_id={"row": r}, device_id_type=MESH,
        )

    def spread_start(buf, send, recv):
        for k in range(1, 8):
            to_col(buf.at[0, 0], buf.at[0, CHIP_BACK[k]], send.at[0], recv.at[0], same[k]).start()

    def spread_seven(buf, send, recv):
        part = buf.at[0, 1:8]
        return to_col(part, part, send.at[0], recv.at[0], twin)

    def spread_twin(buf, send, recv):
        return to_col(buf.at[0], buf.at[1], send.at[1], recv.at[1], twin)

    def reduce_pack(rc, first):
        @each(first, 8)
        def _(k):
            n = rc * 8 + k
            body, diag = pack(terms[table[SRC + n * 2]].astype(F32), terms[table[SRC + n * 2 + 1]].astype(F32))
            mine[rc, k, 0:BLK] = body.astype(BF)
            mine[rc, k, BLK:PACK] = diag.astype(BF)

    def twin_copy(s):
        return to_col(mine.at[1], twins.at[s], x_send.at[s], x_recv.at[s], twin)

    def reduce_send(s):
        twin_copy(s).wait_recv()
        for k in range(7, -1, -1):
            summed[s, k] = (mine[0, k].astype(F32) + twins[s, k].astype(F32)).astype(BF)
            if k:
                to_col(summed.at[s, k], landed.at[s, CHIP_BACK[k]], r_send.at[s], r_recv.at[s], same[k]).start()

    def reduce_seven(s):
        return to_col(summed.at[s, 1:8], landed.at[s, 1:8], r_send.at[s], r_recv.at[s], twin)

    def reduce_end(s):
        reduce_seven(s).wait_recv()
        total = summed[s, 0].astype(F32)
        for k in range(1, 8):
            total = total + landed[s, k].astype(F32)
        sums[s] = total

    def expand(buf, n, m, full, at):
        first, second = unpack(buf[n, m, 0:BLK].astype(F32), buf[n, m, BLK:BLK + 1].astype(F32))
        full[at] = first.astype(BF)
        full[at + 1] = second.astype(BF)

    def expand_half(buf, rc, full):
        @each(0, 8)
        def _(k):
            expand(buf, rc, k, full, (rc * 8 + k) * 2)

    def fold(v):
        return jnp.sum(v.reshape(BLK // 8, 8, BLK), axis=0)

    get_coords.wait()
    own0, own1 = diagonal_slots(coords, me_c)
    load.wait()

    @each(0, TILES)
    def _(t):
        tiles[t] = dens[t].astype(BF)

    zero = jnp.zeros((BLK, BLK), BF)
    tiles[TILES] = zero
    terms[TILES] = zero
    body, diag = pack(tiles[own0].astype(F32), tiles[own1].astype(F32))
    body, diag = body.astype(BF), diag.astype(BF)
    dpack[0, 0, 0:BLK] = body
    dpack[0, 0, BLK:PACK] = diag
    epack[0, 0, 0:BLK] = body
    epack[0, 0, BLK:PACK] = diag

    pl.semaphore_wait(barrier, 21)
    for b in (1, 2, 3):
        to_row(epack.at[0, 0], epack.at[0, RING_BACK[b]], e_send.at[0], ez_recv.at[b // 3], zs[b]).start()

    def along_x(lo, hi, n):
        for a in (1, 2, 3):
            to_row(
                epack.at[0, lo:hi], epack.at[RING_BACK[a], lo:hi], e_send.at[1 + n], ex_recv.at[n], xs[a]
            ).start()

    def ring_wait(part, sem):
        return to_row(part, part, e_send.at[0], sem, me_r)

    along_x(0, 1, 0)

    fill_table(coords, table, which, me_r, me_c, places)

    @each(0, TILES)
    def _(t):
        b = tiles[t]
        terms[t] = dot_t(b, b).astype(BF)

    reduce_pack(1, 0)
    twin_copy(0).start()
    reduce_pack(0, 0)

    reduce_send(0)
    ring_wait(epack.at[0, 1:3], ez_recv.at[0]).wait_recv()
    along_x(1, 3, 0)
    spread_start(dpack, d_send, d_recv)
    ring_wait(epack.at[0, 3], ez_recv.at[1]).wait_recv()
    along_x(3, 4, 1)

    get_lanes.wait()
    flag[0, 0] = any_triple(coords, lanes, me_c)

    reduce_end(0)
    spack[0, 0] = sums[0].astype(BF)

    acc = jnp.zeros((8, BLK), F32)
    row, col = grids()
    parts = []
    for h, s in enumerate(unpack(sums[0, 0:BLK], sums[0, BLK:BLK + 1])):
        d = tiles[own0 if h == 0 else own1]
        rest = s - dot(d, d)
        acc = acc + fold(jnp.where(row == col, 3.0 * s, 0.0) - d.astype(F32) * (4.0 * rest + 2.0 * s))
        parts.append((d, s, rest))
    tcol[0] = acc
    for k in (8, 1, 2, 3, 9, 10, 11, 4, 5, 6, 12, 13, 14, 7, 15):
        back = k // 8 * 8 + CHIP_BACK[k % 8]
        to_col(tcol.at[0], tcol.at[back], t_send.at[0], t_recv.at[0], places[k]).start()
    spread_start(spack, s_send, s_recv)

    for h, (d, s, rest) in enumerate(parts):
        special[h] = 3.0 * s - 2.0 * (dot(d, rest.astype(BF)) + dot(s.astype(BF), d))

    for b in range(4):
        expand(epack, 0, b, efull, b * 2)
    ring_wait(epack.at[1:4, 0:3], ex_recv.at[0]).wait_recv()
    for a in range(1, 4):
        for b in range(3):
            expand(epack, a, b, efull, (a * 4 + b) * 2)
    twin_copy(0).wait_send()
    ring_wait(epack.at[1:4, 3], ex_recv.at[1]).wait_recv()
    for a in range(1, 4):
        expand(epack, a, 3, efull, (a * 4 + 3) * 2)

    @each(0, TILES)
    def _(t):
        b = tiles[t]
        f = dot(b, efull[table[EIDX + t]])
        square[t] = f
        terms[t] = dot_t(f.astype(BF), b).astype(BF)

    reduce_pack(1, 0)
    twin_copy(1).start()
    reduce_pack(0, 1)
    mine[0, 0] = jnp.zeros((PACK, BLK), BF)

    spread_seven(dpack, d_send, d_recv).wait_recv()
    spread_twin(dpack, d_send, d_recv).start()
    expand_half(dpack, 0, dfull)

    tcol_all = to_col(tcol.at[1:16], tcol.at[1:16], t_send.at[0], t_recv.at[0], twin)
    tcol_all.wait_recv()
    tz[0] = jnp.sum(tcol[...], axis=0)
    for b in (1, 2, 3):
        to_row(tz.at[0], tz.at[RING_BACK[b]], t_send.at[1], t_recv.at[1], zs[b]).start()

    reduce_send(1)

    spread_twin(dpack, d_send, d_recv).wait_recv()
    expand_half(dpack, 1, dfull)

    @each(0, TILES)
    def _(t):
        s = square[t] + dot(dfull[table[DIDX + t]], tiles[t])
        outs[t] = 3.0 * s - 2.0 * dot(s.astype(BF), efull[table[EIDX + t]])

    spread_seven(spack, s_send, s_recv).wait_recv()
    spread_twin(spack, s_send, s_recv).start()
    expand_half(spack, 0, sfull)

    tz_three = to_row(tz.at[1:4], tz.at[1:4], t_send.at[1], t_recv.at[1], me_r)
    tz_three.wait_recv()
    tx[0] = jnp.sum(tz[...], axis=0)
    for a in (1, 2, 3):
        to_row(tx.at[0], tx.at[RING_BACK[a]], t_send.at[2], t_recv.at[2], xs[a]).start()

    spread_twin(spack, s_send, s_recv).wait_recv()
    expand_half(spack, 1, sfull)

    @each(0, TILES)
    def _(t):
        outs[t] = outs[t] - 2.0 * dot(sfull[table[DIDX + t]], tiles[t])

    store = pltpu.make_async_copy(outs, out_hbm, out_sem)
    store.start()

    reduce_end(1)
    for h, q in enumerate(unpack(sums[1, 0:BLK], sums[1, BLK:BLK + 1])):
        special[h] = special[h] - 2.0 * q

    for buf, send, recv in ((dpack, d_send, d_recv), (spack, s_send, s_recv)):
        spread_seven(buf, send, recv).wait_send()
        spread_twin(buf, send, recv).wait_send()
    ring_wait(epack.at[0, 1:4], ez_recv.at[0]).wait_send()
    part = epack.at[1:4, 0:3]
    to_row(part, part, e_send.at[1], ex_recv.at[0], me_r).wait_send()
    part = epack.at[1:4, 3]
    to_row(part, part, e_send.at[2], ex_recv.at[1], me_r).wait_send()
    twin_copy(1).wait_send()
    reduce_seven(0).wait_send()
    reduce_seven(1).wait_send()
    tcol_all.wait_send()
    tz_three.wait_send()

    tx_three = to_row(tx.at[1:4], tx.at[1:4], t_send.at[2], t_recv.at[2], me_r)
    tx_three.wait_recv()
    trace[0, 0] = jnp.sum(tx[...]) / (NB * BLK)
    tx_three.wait_send()
    store.wait()


def fast_call(coords, dens):
    dma = pltpu.SemaphoreType.DMA
    pair = (2, 8, PACK, BLK)
    smem = pl.BlockSpec(memory_space=pltpu.SMEM)
    return pl.pallas_call(
        kernel,
        out_shape=(
            jax.ShapeDtypeStruct((TILES, BLK, BLK), F32),
            jax.ShapeDtypeStruct((2, BLK, BLK), F32),
            jax.ShapeDtypeStruct((1, 1), F32),
            jax.ShapeDtypeStruct((1, 1), jnp.int32),
            jax.ShapeDtypeStruct((TILES,), jnp.int32),
        ),
        in_specs=[pl.BlockSpec(memory_space=pl.ANY), pl.BlockSpec(memory_space=pl.ANY)],
        out_specs=(
            pl.BlockSpec(memory_space=pl.ANY), pl.BlockSpec(memory_space=pltpu.VMEM), smem, smem, smem,
        ),
        scratch_shapes=[
            pltpu.SMEM((16, 2, TILES), jnp.int32),
            pltpu.SMEM((TABLE,), jnp.int32),
            pltpu.VMEM((2, TILES), jnp.int32),
            pltpu.VMEM((TILES, BLK, BLK), F32),
            pltpu.VMEM((TILES + 1, BLK, BLK), BF),
            pltpu.VMEM((TILES + 1, BLK, BLK), BF),
            pltpu.VMEM(pair, BF),
            pltpu.VMEM((4, 4, PACK, BLK), BF),
            pltpu.VMEM(pair, BF),
            pltpu.VMEM(pair, BF),
            pltpu.VMEM(pair, BF),
            pltpu.VMEM(pair, BF),
            pltpu.VMEM(pair, BF),
            pltpu.VMEM((2, PACK, BLK), F32),
            pltpu.VMEM((32, BLK, BLK), BF),
            pltpu.VMEM((32, BLK, BLK), BF),
            pltpu.VMEM((32, BLK, BLK), BF),
            pltpu.VMEM((TILES, BLK, BLK), F32),
            pltpu.VMEM((TILES, BLK, BLK), F32),
            pltpu.VMEM((16, 8, BLK), F32),
            pltpu.VMEM((4, 8, BLK), F32),
            pltpu.VMEM((4, 8, BLK), F32),
            dma((3,)),
            dma((2,)), dma((2,)),
            dma((3,)), dma((2,)), dma((2,)),
            dma((2,)), dma((2,)),
            dma((2,)), dma((2,)),
            dma((2,)), dma((2,)),
            dma((3,)), dma((3,)),
            dma(()),
        ],
        compiler_params=pltpu.CompilerParams(
            collective_id=0, has_side_effects=True, vmem_limit_bytes=40 * 1024 * 1024
        ),
    )(coords, dens)


def pair_lookup(own_coords, targets, mirror_coords):
    own_rows = own_coords[:, 0]
    own_cols = own_coords[:, 1]
    target_row = targets[:, 0]
    target_col = targets[:, 1]
    first = own_rows[None, :] == target_row[:, None]
    has_first = jnp.any(first, axis=1)
    left_slot = jnp.argmax(first.astype(jnp.int32), axis=1)
    inner = own_cols[left_slot]
    second = (mirror_coords[None, :, 0] == target_col[:, None]) & (
        mirror_coords[None, :, 1] == inner[:, None]
    )
    second = second & has_first[:, None]
    keep = jnp.any(second, axis=1)
    right_slot = jnp.argmax(second.astype(jnp.int32), axis=1)
    return (left_slot, right_slot, keep)


def to_all(value, axis):
    return lax.all_to_all(jnp.broadcast_to(value[None], (16,) + value.shape), axis, 0, 0)


def scattered_product(left, mirror, left_slot, right_slot, keep):
    weight = keep.astype(F32)
    left_rows = jnp.take(left, left_slot, axis=0)
    right_rows = jnp.take(mirror, right_slot, axis=0)
    result = jnp.einsum("nik,njk->nij", left_rows, right_rows, preferred_element_type=F32)
    result = (result * weight[:, None, None]).astype(BF).reshape(16, TILES, BLK, BLK)
    return jnp.sum(lax.all_to_all(result, "col", 0, 0).astype(F32), axis=0)


def general(density, tile_coords):
    own_tiles = density[0, 0]
    own_low = own_tiles.astype(BF)
    my_row = lax.axis_index("row")
    my_col = lax.axis_index("col")
    row_table = jnp.take(tile_coords, my_row, axis=0)
    own_coords = jnp.take(row_table, my_col, axis=0)
    row_flat = row_table.reshape(-1, 2)
    col_flat = jnp.take(tile_coords, my_col, axis=1).reshape(-1, 2)
    mirror = to_all(own_low, "row").reshape(-1, BLK, BLK)
    own_diag = own_coords[:, 0] == own_coords[:, 1]
    left_slot, right_slot, keep = pair_lookup(own_coords, row_flat, col_flat)
    square = scattered_product(own_low, mirror, left_slot, right_slot, keep)
    square_low = square.astype(BF)
    cube = scattered_product(square_low, mirror, left_slot, right_slot, keep)
    purified = 3.0 * square - 2.0 * cube
    total = jnp.sum(jnp.where(own_diag, jnp.einsum("nii->n", purified), 0.0))
    total = jnp.sum(to_all(jnp.sum(to_all(total, "col")), "row"))
    return purified, total / (NB * BLK)


def per_device(density, tile_coords):
    out, special, trace, flag, which = fast_call(tile_coords.transpose(0, 1, 3, 2), density[0, 0])
    which = which[:, None, None]
    out = jnp.where(which == 0, out, jnp.where(which == 1, special[0][None], special[1][None]))
    out, mean_diagonal = lax.cond(
        flag[0, 0] > 0,
        lambda out, trace: general(density, tile_coords),
        lambda out, trace: (out, trace),
        out, trace[0, 0],
    )
    return out[None, None], mean_diagonal


def solution(mesh):
    return jax.shard_map(
        per_device,
        mesh=mesh,
        in_specs=(P("row", "col", None, None, None), P()),
        out_specs=(P("row", "col", None, None, None), P()),
        check_vma=False,
    )
```

```python
import jax
import jax.numpy as jnp
from jax import lax
from jax.experimental import pallas as pl
from jax.experimental.pallas import tpu as pltpu
from jax.sharding import PartitionSpec as P

NB = 512
BLK = 128
TILES = 18
PACK = BLK + 16
BF = jnp.bfloat16
F32 = jnp.float32
MESH = pl.DeviceIdType.MESH

CHIP_STEPS = ((0, 0), (0, 1), (0, 3), (1, 0), (0, 2), (1, 1), (1, 3), (1, 2))
CHIP_BACK = tuple(CHIP_STEPS.index((-dz % 2, -dy % 4)) for dz, dy in CHIP_STEPS)
RING = (0, 1, 3, 2)
RING_BACK = tuple(RING.index(-d % 4) for d in RING)

SRC, DIDX, EIDX, TABLE = 0, 32, 64, 96


def dot(a, b):
    return jnp.dot(a, b, preferred_element_type=F32)


def dot_t(a, b):
    return lax.dot_general(a, b, (((1,), (1,)), ((), ())), preferred_element_type=F32)


def each(lo, hi):
    return pl.loop(lo, hi, unroll=True)


def grids():
    row = lax.broadcasted_iota(jnp.int32, (BLK, BLK), 0)
    col = lax.broadcasted_iota(jnp.int32, (BLK, BLK), 1)
    return row, col


def pack(first, second):
    row, col = grids()
    body = jnp.where(row <= col, first, second)
    diag = jnp.sum(jnp.where(row == col, second, 0.0), axis=0, keepdims=True)
    return body, jnp.broadcast_to(diag, (PACK - BLK, BLK))


def unpack(body, diag):
    row, col = grids()
    turned = body.T
    first = jnp.where(row <= col, body, turned)
    second = jnp.where(row > col, body, jnp.where(row < col, turned, diag))
    return first, second


def fill_table(coords, table, which, me_r, me_c, places):
    classes = [coords[c, 1, 0] & 15 for c in places]
    zhi, x = me_r // 4, lax.rem(me_r, 4)
    keys = []
    for t in range(TILES):
        i, j = coords[me_c, 0, t], coords[me_c, 1, t]
        residue, half = i & 15, i >> 8
        place = jnp.int32(0)
        for n in range(16):
            place = jnp.where(classes[n] == residue, n, place)
        key = place * 2 + half
        keys.append(key)
        table[DIDX + t] = key
        dz, dx = ((j >> 6) - zhi) & 3, ((j >> 4) - x) & 3
        table[EIDX + t] = ((dx ^ (dx >> 1)) * 4 + (dz ^ (dz >> 1))) * 2 + (j >> 8)
        which[t] = jnp.where(i == j, 1 + half, 0)
    for n in range(32):
        slot = jnp.int32(TILES)
        for t in range(TILES):
            slot = jnp.where(keys[t] == n, t, slot)
        table[SRC + n] = slot


def diagonal_slots(coords, me_c):
    first, second = jnp.int32(0), jnp.int32(0)
    for t in range(TILES):
        i, j = coords[me_c, 0, t], coords[me_c, 1, t]
        first = jnp.where(jnp.logical_and(i == j, i < NB // 2), t, first)
        second = jnp.where(jnp.logical_and(i == j, i >= NB // 2), t, second)
    return first, second


def any_triple(coords, lanes, me_c):
    wide = (lanes[1:2] - lanes[0:1]) & (NB - 1)
    wide = jnp.where(wide == 0, -2, wide)
    offsets = [(coords[me_c, 1, t] - coords[me_c, 0, t]) & (NB - 1) for t in range(TILES)]
    found = jnp.zeros(wide.shape, jnp.int32)
    for s in range(TILES):
        for t in range(s, TILES):
            live = jnp.logical_and(offsets[s] != 0, offsets[t] != 0)
            both = jnp.where(live, (offsets[s] + offsets[t]) & (NB - 1), -1)
            found = found | (wide == both).astype(jnp.int32)
    return jnp.max(found)


def kernel(
    coords_hbm, dens_hbm, out_hbm, special, trace, flag, which,
    coords, table, lanes, dens, tiles, terms, dpack, epack, spack, mine, twins, summed, landed, sums,
    dfull, efull, sfull, square, outs, tcol, tz, tx,
    load_sem, d_send, d_recv, e_send, ez_recv, ex_recv, s_send, s_recv,
    x_send, x_recv, r_send, r_recv, t_send, t_recv, out_sem,
):
    me_r = lax.axis_index("row")
    me_c = lax.axis_index("col")
    core = lax.rem(me_c, 2)
    chip = me_c // 2
    zlo, y = chip // 4, lax.rem(chip, 4)
    zhi, x = me_r // 4, lax.rem(me_r, 4)
    chips = [lax.rem(zlo + dz, 2) * 4 + lax.rem(y + dy, 4) for dz, dy in CHIP_STEPS]
    same = [ch * 2 + core for ch in chips]
    places = same + [ch * 2 + 1 - core for ch in chips]
    twin = places[8]
    zs = [lax.rem(zhi + d, 4) * 4 + x for d in RING]
    xs = [zhi * 4 + lax.rem(x + d, 4) for d in RING]

    barrier = pltpu.get_barrier_semaphore()
    get_coords = pltpu.make_async_copy(coords_hbm.at[me_r], coords, load_sem.at[0])
    load = pltpu.make_async_copy(dens_hbm, dens, load_sem.at[1])
    get_lanes = pltpu.make_async_copy(coords_hbm.at[me_r, me_c], lanes, load_sem.at[2])
    get_coords.start()
    load.start()
    for b in (3, 2, 1):
        pl.semaphore_signal(barrier, inc=1, device_id={"row": zs[b]}, device_id_type=MESH)
    for n in range(15, 0, -1):
        pl.semaphore_signal(barrier, inc=1, device_id={"col": places[n]}, device_id_type=MESH)
    for a in (3, 2, 1):
        pl.semaphore_signal(barrier, inc=1, device_id={"row": xs[a]}, device_id_type=MESH)
    get_lanes.start()

    def to_col(src, dst, send, recv, c):
        return pltpu.make_async_remote_copy(
            src_ref=src, dst_ref=dst, send_sem=send, recv_sem=recv,
            device_id={"col": c}, device_id_type=MESH,
        )

    def to_row(src, dst, send, recv, r):
        return pltpu.make_async_remote_copy(
            src_ref=src, dst_ref=dst, send_sem=send, recv_sem=recv,
            device_id={"row": r}, device_id_type=MESH,
        )

    def spread_start(buf, send, recv):
        for k in range(1, 8):
            to_col(buf.at[0, 0], buf.at[0, CHIP_BACK[k]], send.at[0], recv.at[0], same[k]).start()

    def spread_seven(buf, send, recv):
        part = buf.at[0, 1:8]
        return to_col(part, part, send.at[0], recv.at[0], twin)

    def spread_twin(buf, send, recv):
        return to_col(buf.at[0], buf.at[1], send.at[1], recv.at[1], twin)

    def reduce_pack(rc, first):
        @each(first, 8)
        def _(k):
            n = rc * 8 + k
            body, diag = pack(terms[table[SRC + n * 2]].astype(F32), terms[table[SRC + n * 2 + 1]].astype(F32))
            mine[rc, k, 0:BLK] = body.astype(BF)
            mine[rc, k, BLK:PACK] = diag.astype(BF)

    def twin_copy(s):
        return to_col(mine.at[1], twins.at[s], x_send.at[s], x_recv.at[s], twin)

    def reduce_send(s):
        twin_copy(s).wait_recv()
        for k in range(7, -1, -1):
            summed[s, k] = (mine[0, k].astype(F32) + twins[s, k].astype(F32)).astype(BF)
            if k:
                to_col(summed.at[s, k], landed.at[s, CHIP_BACK[k]], r_send.at[s], r_recv.at[s], same[k]).start()

    def reduce_seven(s):
        return to_col(summed.at[s, 1:8], landed.at[s, 1:8], r_send.at[s], r_recv.at[s], twin)

    def reduce_end(s):
        reduce_seven(s).wait_recv()
        total = summed[s, 0].astype(F32)
        for k in range(1, 8):
            total = total + landed[s, k].astype(F32)
        sums[s] = total

    def expand(buf, n, m, full, at):
        first, second = unpack(buf[n, m, 0:BLK].astype(F32), buf[n, m, BLK:BLK + 1].astype(F32))
        full[at] = first.astype(BF)
        full[at + 1] = second.astype(BF)

    def expand_half(buf, rc, full):
        @each(0, 8)
        def _(k):
            expand(buf, rc, k, full, (rc * 8 + k) * 2)

    def fold(v):
        return jnp.sum(v.reshape(BLK // 8, 8, BLK), axis=0)

    get_coords.wait()
    own0, own1 = diagonal_slots(coords, me_c)
    load.wait()

    @each(0, TILES)
    def _(t):
        tiles[t] = dens[t].astype(BF)

    zero = jnp.zeros((BLK, BLK), BF)
    tiles[TILES] = zero
    terms[TILES] = zero
    body, diag = pack(tiles[own0].astype(F32), tiles[own1].astype(F32))
    body, diag = body.astype(BF), diag.astype(BF)
    dpack[0, 0, 0:BLK] = body
    dpack[0, 0, BLK:PACK] = diag
    epack[0, 0, 0:BLK] = body
    epack[0, 0, BLK:PACK] = diag

    pl.semaphore_wait(barrier, 21)
    for b in (1, 2, 3):
        to_row(epack.at[0, 0], epack.at[0, RING_BACK[b]], e_send.at[0], ez_recv.at[b // 3], zs[b]).start()

    def along_x(lo, hi, n):
        for a in (1, 2, 3):
            to_row(
                epack.at[0, lo:hi], epack.at[RING_BACK[a], lo:hi], e_send.at[1 + n], ex_recv.at[n], xs[a]
            ).start()

    def ring_wait(part, sem):
        return to_row(part, part, e_send.at[0], sem, me_r)

    along_x(0, 1, 0)

    fill_table(coords, table, which, me_r, me_c, places)

    @each(0, TILES)
    def _(t):
        b = tiles[t]
        terms[t] = dot_t(b, b).astype(BF)

    reduce_pack(1, 0)
    twin_copy(0).start()
    reduce_pack(0, 0)

    reduce_send(0)
    ring_wait(epack.at[0, 1:3], ez_recv.at[0]).wait_recv()
    along_x(1, 3, 0)
    spread_start(dpack, d_send, d_recv)
    ring_wait(epack.at[0, 3], ez_recv.at[1]).wait_recv()
    along_x(3, 4, 1)

    get_lanes.wait()
    flag[0, 0] = any_triple(coords, lanes, me_c)

    reduce_end(0)
    spack[0, 0] = sums[0].astype(BF)

    acc = jnp.zeros((8, BLK), F32)
    row, col = grids()
    parts = []
    for h, s in enumerate(unpack(sums[0, 0:BLK], sums[0, BLK:BLK + 1])):
        d = tiles[own0 if h == 0 else own1]
        rest = s - dot(d, d)
        acc = acc + fold(jnp.where(row == col, 3.0 * s, 0.0) - d.astype(F32) * (4.0 * rest + 2.0 * s))
        parts.append((d, s, rest))
    tcol[0] = acc
    for k in (8, 1, 2, 3, 9, 10, 11, 4, 5, 6, 12, 13, 14, 7, 15):
        back = k // 8 * 8 + CHIP_BACK[k % 8]
        to_col(tcol.at[0], tcol.at[back], t_send.at[0], t_recv.at[0], places[k]).start()
    spread_start(spack, s_send, s_recv)

    for h, (d, s, rest) in enumerate(parts):
        special[h] = 3.0 * s - 2.0 * (dot(d, rest.astype(BF)) + dot(s.astype(BF), d))

    for b in range(4):
        expand(epack, 0, b, efull, b * 2)
    ring_wait(epack.at[1:4, 0:3], ex_recv.at[0]).wait_recv()
    for a in range(1, 4):
        for b in range(3):
            expand(epack, a, b, efull, (a * 4 + b) * 2)
    twin_copy(0).wait_send()
    ring_wait(epack.at[1:4, 3], ex_recv.at[1]).wait_recv()
    for a in range(1, 4):
        expand(epack, a, 3, efull, (a * 4 + 3) * 2)

    @each(0, TILES)
    def _(t):
        b = tiles[t]
        f = dot(b, efull[table[EIDX + t]])
        square[t] = f
        terms[t] = dot_t(f.astype(BF), b).astype(BF)

    reduce_pack(1, 0)
    twin_copy(1).start()
    reduce_pack(0, 1)
    mine[0, 0] = jnp.zeros((PACK, BLK), BF)

    spread_seven(dpack, d_send, d_recv).wait_recv()
    spread_twin(dpack, d_send, d_recv).start()
    expand_half(dpack, 0, dfull)

    tcol_all = to_col(tcol.at[1:16], tcol.at[1:16], t_send.at[0], t_recv.at[0], twin)
    tcol_all.wait_recv()
    tz[0] = jnp.sum(tcol[...], axis=0)
    for b in (1, 2, 3):
        to_row(tz.at[0], tz.at[RING_BACK[b]], t_send.at[1], t_recv.at[1], zs[b]).start()

    reduce_send(1)

    spread_twin(dpack, d_send, d_recv).wait_recv()
    expand_half(dpack, 1, dfull)

    @each(0, TILES)
    def _(t):
        s = square[t] + dot(dfull[table[DIDX + t]], tiles[t])
        outs[t] = 3.0 * s - 2.0 * dot(s.astype(BF), efull[table[EIDX + t]])

    spread_seven(spack, s_send, s_recv).wait_recv()
    spread_twin(spack, s_send, s_recv).start()
    expand_half(spack, 0, sfull)

    tz_three = to_row(tz.at[1:4], tz.at[1:4], t_send.at[1], t_recv.at[1], me_r)
    tz_three.wait_recv()
    tx[0] = jnp.sum(tz[...], axis=0)
    for a in (1, 2, 3):
        to_row(tx.at[0], tx.at[RING_BACK[a]], t_send.at[2], t_recv.at[2], xs[a]).start()

    spread_twin(spack, s_send, s_recv).wait_recv()
    expand_half(spack, 1, sfull)

    @each(0, TILES)
    def _(t):
        outs[t] = outs[t] - 2.0 * dot(sfull[table[DIDX + t]], tiles[t])

    store = pltpu.make_async_copy(outs, out_hbm, out_sem)
    store.start()

    reduce_end(1)
    for h, q in enumerate(unpack(sums[1, 0:BLK], sums[1, BLK:BLK + 1])):
        special[h] = special[h] - 2.0 * q

    for buf, send, recv in ((dpack, d_send, d_recv), (spack, s_send, s_recv)):
        spread_seven(buf, send, recv).wait_send()
        spread_twin(buf, send, recv).wait_send()
    ring_wait(epack.at[0, 1:4], ez_recv.at[0]).wait_send()
    part = epack.at[1:4, 0:3]
    to_row(part, part, e_send.at[1], ex_recv.at[0], me_r).wait_send()
    part = epack.at[1:4, 3]
    to_row(part, part, e_send.at[2], ex_recv.at[1], me_r).wait_send()
    twin_copy(1).wait_send()
    reduce_seven(0).wait_send()
    reduce_seven(1).wait_send()
    tcol_all.wait_send()
    tz_three.wait_send()

    tx_three = to_row(tx.at[1:4], tx.at[1:4], t_send.at[2], t_recv.at[2], me_r)
    tx_three.wait_recv()
    trace[0, 0] = jnp.sum(tx[...]) / (NB * BLK)
    tx_three.wait_send()
    store.wait()


def fast_call(coords, dens):
    dma = pltpu.SemaphoreType.DMA
    pair = (2, 8, PACK, BLK)
    smem = pl.BlockSpec(memory_space=pltpu.SMEM)
    return pl.pallas_call(
        kernel,
        out_shape=(
            jax.ShapeDtypeStruct((TILES, BLK, BLK), F32),
            jax.ShapeDtypeStruct((2, BLK, BLK), F32),
            jax.ShapeDtypeStruct((1, 1), F32),
            jax.ShapeDtypeStruct((1, 1), jnp.int32),
            jax.ShapeDtypeStruct((TILES,), jnp.int32),
        ),
        in_specs=[pl.BlockSpec(memory_space=pl.ANY), pl.BlockSpec(memory_space=pl.ANY)],
        out_specs=(
            pl.BlockSpec(memory_space=pl.ANY), pl.BlockSpec(memory_space=pltpu.VMEM), smem, smem, smem,
        ),
        scratch_shapes=[
            pltpu.SMEM((16, 2, TILES), jnp.int32),
            pltpu.SMEM((TABLE,), jnp.int32),
            pltpu.VMEM((2, TILES), jnp.int32),
            pltpu.VMEM((TILES, BLK, BLK), F32),
            pltpu.VMEM((TILES + 1, BLK, BLK), BF),
            pltpu.VMEM((TILES + 1, BLK, BLK), BF),
            pltpu.VMEM(pair, BF),
            pltpu.VMEM((4, 4, PACK, BLK), BF),
            pltpu.VMEM(pair, BF),
            pltpu.VMEM(pair, BF),
            pltpu.VMEM(pair, BF),
            pltpu.VMEM(pair, BF),
            pltpu.VMEM(pair, BF),
            pltpu.VMEM((2, PACK, BLK), F32),
            pltpu.VMEM((32, BLK, BLK), BF),
            pltpu.VMEM((32, BLK, BLK), BF),
            pltpu.VMEM((32, BLK, BLK), BF),
            pltpu.VMEM((TILES, BLK, BLK), F32),
            pltpu.VMEM((TILES, BLK, BLK), F32),
            pltpu.VMEM((16, 8, BLK), F32),
            pltpu.VMEM((4, 8, BLK), F32),
            pltpu.VMEM((4, 8, BLK), F32),
            dma((3,)),
            dma((2,)), dma((2,)),
            dma((3,)), dma((2,)), dma((2,)),
            dma((2,)), dma((2,)),
            dma((2,)), dma((2,)),
            dma((2,)), dma((2,)),
            dma((3,)), dma((3,)),
            dma(()),
        ],
        compiler_params=pltpu.CompilerParams(
            collective_id=0, has_side_effects=True, vmem_limit_bytes=40 * 1024 * 1024
        ),
    )(coords, dens)


def gather_kernel(own, out, move_sem, z_send, z_recv, x_send, x_recv):
    me_r = lax.axis_index("row")
    zhi, x = me_r // 4, lax.rem(me_r, 4)
    zs = [lax.rem(zhi + d, 4) * 4 + x for d in RING]
    xs = [zhi * 4 + lax.rem(x + d, 4) for d in RING]
    barrier = pltpu.get_barrier_semaphore()
    for n in range(1, 4):
        pl.semaphore_signal(barrier, inc=1, device_id={"row": zs[n]}, device_id_type=MESH)
        pl.semaphore_signal(barrier, inc=1, device_id={"row": xs[n]}, device_id_type=MESH)
    move = pltpu.make_async_copy(own, out.at[0, 0], move_sem)
    move.start()
    pl.semaphore_wait(barrier, 6)

    def along(src, dst, send, recv, r):
        return pltpu.make_async_remote_copy(
            src_ref=src, dst_ref=dst, send_sem=send, recv_sem=recv,
            device_id={"row": r}, device_id_type=MESH,
        )

    for b in range(1, 4):
        along(own, out.at[0, RING_BACK[b]], z_send.at[b], z_recv.at[RING_BACK[b]], zs[b]).start()
    for a in range(1, 4):
        along(own, out.at[RING_BACK[a], 0], x_send.at[a, 0], x_recv.at[RING_BACK[a], 0], xs[a]).start()
    for b in range(1, 4):
        part = out.at[0, b]
        along(part, part, z_send.at[b], z_recv.at[b], me_r).wait_recv()
        for a in range(1, 4):
            along(part, out.at[RING_BACK[a], b], x_send.at[a, b], x_recv.at[RING_BACK[a], b], xs[a]).start()
    for b in range(4):
        for a in range(1, 4):
            part = out.at[a, b]
            along(part, part, x_send.at[a, b], x_recv.at[a, b], me_r).wait_recv()
    for b in range(1, 4):
        along(own, own, z_send.at[b], z_recv.at[b], me_r).wait_send()
    for b in range(4):
        for a in range(1, 4):
            along(own, own, x_send.at[a, b], x_recv.at[a, b], me_r).wait_send()
    move.wait()


def gather_column_class(own):
    dma = pltpu.SemaphoreType.DMA
    return pl.pallas_call(
        gather_kernel,
        out_shape=jax.ShapeDtypeStruct((4, 4) + own.shape, own.dtype),
        in_specs=[pl.BlockSpec(memory_space=pl.ANY)],
        out_specs=pl.BlockSpec(memory_space=pl.ANY),
        scratch_shapes=[dma(()), dma((4,)), dma((4,)), dma((4, 4)), dma((4, 4))],
        compiler_params=pltpu.CompilerParams(collective_id=1, has_side_effects=True),
    )(own)


def pair_lookup(own_coords, targets, mirror_coords):
    own_rows = own_coords[:, 0]
    own_cols = own_coords[:, 1]
    target_row = targets[:, 0]
    target_col = targets[:, 1]
    first = own_rows[None, :] == target_row[:, None]
    has_first = jnp.any(first, axis=1)
    left_slot = jnp.argmax(first.astype(jnp.int32), axis=1)
    inner = own_cols[left_slot]
    second = (mirror_coords[None, :, 0] == target_col[:, None]) & (
        mirror_coords[None, :, 1] == inner[:, None]
    )
    second = second & has_first[:, None]
    keep = jnp.any(second, axis=1)
    right_slot = jnp.argmax(second.astype(jnp.int32), axis=1)
    return (left_slot, right_slot, keep)


def to_all(value, axis):
    return lax.all_to_all(jnp.broadcast_to(value[None], (16,) + value.shape), axis, 0, 0)


def scattered_product(left, mirror, left_slot, right_slot, keep):
    weight = keep.astype(F32)
    left_rows = jnp.take(left, left_slot, axis=0)
    right_rows = jnp.take(mirror, right_slot, axis=0)
    result = jnp.einsum("nik,njk->nij", left_rows, right_rows, preferred_element_type=F32)
    result = (result * weight[:, None, None]).astype(BF).reshape(16, TILES, BLK, BLK)
    return jnp.sum(lax.all_to_all(result, "col", 0, 0).astype(F32), axis=0)


def general(density, tile_coords):
    own_tiles = density[0, 0]
    own_low = own_tiles.astype(BF)
    my_row = lax.axis_index("row")
    my_col = lax.axis_index("col")
    row_table = jnp.take(tile_coords, my_row, axis=0)
    own_coords = jnp.take(row_table, my_col, axis=0)
    row_flat = row_table.reshape(-1, 2)
    zhi, x = my_row // 4, my_row % 4
    order = jnp.stack([(zhi + b) % 4 * 4 + (x + a) % 4 for a in RING for b in RING])
    col_flat = jnp.take(jnp.take(tile_coords, my_col, axis=1), order, axis=0).reshape(-1, 2)
    mirror = gather_column_class(own_low).reshape(-1, BLK, BLK)
    own_diag = own_coords[:, 0] == own_coords[:, 1]
    left_slot, right_slot, keep = pair_lookup(own_coords, row_flat, col_flat)
    square = scattered_product(own_low, mirror, left_slot, right_slot, keep)
    square_low = square.astype(BF)
    cube = scattered_product(square_low, mirror, left_slot, right_slot, keep)
    purified = 3.0 * square - 2.0 * cube
    total = jnp.sum(jnp.where(own_diag, jnp.einsum("nii->n", purified), 0.0))
    total = jnp.sum(to_all(jnp.sum(to_all(total, "col")), "row"))
    return purified, total / (NB * BLK)


def per_device(density, tile_coords):
    out, special, trace, flag, which = fast_call(tile_coords.transpose(0, 1, 3, 2), density[0, 0])
    which = which[:, None, None]
    out = jnp.where(which == 0, out, jnp.where(which == 1, special[0][None], special[1][None]))
    out, mean_diagonal = lax.cond(
        flag[0, 0] > 0,
        lambda out, trace: general(density, tile_coords),
        lambda out, trace: (out, trace),
        out, trace[0, 0],
    )
    return out[None, None], mean_diagonal


def solution(mesh):
    return jax.shard_map(
        per_device,
        mesh=mesh,
        in_specs=(P("row", "col", None, None, None), P()),
        out_specs=(P("row", "col", None, None, None), P()),
        check_vma=False,
    )
```
